256 devices in a mesh: row: 16 (over x, z_hi, core), col: 16 (over z_lo, y).
Axes of the slice: x: 4, y: 4, z: 8 (z_hi: 2, z_lo: 4; z = z_hi * 4 + z_lo), core: 2. Of those that a mesh axis runs over, the one named last changes fastest.
Arguments:
- pair_valence: bfloat16 [1792, 2048], P('row'), may hold values from -0.125 to 0.125
- screening: bfloat16 [1792, 1792], P('row', 'col'), may hold values from -0.125 to 0.125
- pair_conduction: bfloat16 [1792, 98304], P(None, ('row', 'col')), may hold values from -6 to 6
Outputs:
- kernel: bfloat16 [2048, 98304], P(None, ('row', 'col'))
The draws below stay inside these ranges and needn't reach their ends.
All inputs are finite; a program needn't handle non-finite values.
Results may differ from the reference program's by a relative error of at most 0.015.
Values may be sent and summed in bfloat16 or wider, within the bound.
No kernel may reach another device: no remote copies, remote signals or barrier semaphores. Data moves between devices by JAX's collectives and lax.ppermute only.
A program may use at most 64 MiB of HBM per device.

```python
import jax
import jax.numpy as jnp
from jax import lax

NG = 1792
PR = 2048
CD = 384
PC = 98304


def steps_of(own_key, dims, shards, least, high):
    def one(dim, shards_of):
        draws = jax.random.uniform(jax.random.fold_in(jax.random.fold_in(own_key, 6), dim), (shards_of,), jnp.float32, least / len(shards), high / len(shards))
        return jnp.repeat(jnp.exp(draws), dims[dim] // shards_of).reshape((-1,) + (1,) * (len(dims) - dim - 1))

    level = one(*shards[0])
    for cut in shards[1:]:
        level = level * one(*cut)
    return level


def scatter_about(rng, dims, scale, most, cuts=(), dtype=jnp.bfloat16):
    level = steps_of(rng, dims, cuts, -0.22, 0.18) if cuts else 1.0
    array = jax.random.normal(rng, dims, jnp.float32) * scale * level
    return jnp.minimum(jnp.maximum(array, -most), most).astype(dtype)


def setup_inputs(seed: int = 0) -> dict:
    arg_keys = jax.random.split(jax.random.key(seed), 4)
    pair_valence = scatter_about(arg_keys[0], (NG, PR), NG ** -0.5, 0.125, ((0, 16),))
    screening = scatter_about(arg_keys[1], (NG, NG), NG ** -0.5, 0.125, ((0, 16), (1, 16)))
    pair_conduction = scatter_about(arg_keys[2], (NG, PC), 1.0, 6.0, ((1, 256),))
    return dict(pair_valence=pair_valence, screening=screening, pair_conduction=pair_conduction)


def reference(pair_valence, screening, pair_conduction):
    blocks = pair_conduction.reshape(NG, PC // CD, CD).transpose(1, 0, 2)

    def block_kernel(columns):
        screened = jnp.dot(screening, columns, preferred_element_type=jnp.float32).astype(jnp.bfloat16)
        return lax.dot_general(pair_valence, screened, (((0,), (0,)), ((), ())), preferred_element_type=jnp.float32)

    tiles = lax.map(block_kernel, blocks)
    return tiles.transpose(1, 0, 2).reshape(PR, PC).astype(jnp.bfloat16)
```

```python
import jax
import jax.numpy as jnp
from jax import lax
from jax.sharding import Mesh, PartitionSpec as P

ROW = ("x", "z_hi", "core")
COL = ("z_lo", "y")
Z = ("z_hi", "z_lo")
BF16 = jnp.bfloat16
F32 = jnp.float32


def fetch(block, axis, size, ahead):
    return lax.ppermute(block, axis, [((i + ahead) % size, i) for i in range(size)])


def gather(block, axis, size):
    return [block] + [fetch(block, axis, size, ahead) for ahead in range(1, size)]


def in_order(blocks, me):
    size = len(blocks)
    twice = jnp.concatenate([jnp.stack(blocks)] * 2)
    return lax.dynamic_slice_in_dim(twice, size - me, size)


def ring4(block, axis):
    after = fetch(block, axis, 4, 1)
    before = fetch(block, axis, 4, -1)
    half = block.shape[0] // 2
    far = [fetch(after[:half], axis, 4, 1), fetch(before[half:], axis, 4, -1)]
    return [block, after, jnp.concatenate(far), before]


def pick(stack, index):
    return lax.dynamic_index_in_dim(stack, index, 0, keepdims=False)


def per_device(pair_valence, screening, pair_conduction):
    x, y = lax.axis_index("x"), lax.axis_index("y")
    z_hi, z_lo, core = lax.axis_index("z_hi"), lax.axis_index("z_lo"), lax.axis_index("core")
    pairs_other = fetch(pair_conduction, "core", 2, 1)

    some = in_order(gather(screening.T, "y", 4), y)
    columns = in_order(gather(some, "z_lo", 4), z_lo).reshape(1792, 112)

    panel = lax.dynamic_slice_in_dim(pair_valence, (y * 4 + z_lo) * 128, 128, 1)
    part = lax.dot_general(panel, columns, (((0,), (1,)), ((), ())), preferred_element_type=F32)

    part = part.reshape(2, 64, 1792)
    part = pick(part, core) + fetch(pick(part, 1 - core), "core", 2, 1)
    part = part.reshape(4, 16, 1792)
    part = pick(part, x) + sum(
        fetch(pick(part, (x + 4 - ahead) % 4), "x", 4, ahead) for ahead in (1, 2, 3)
    )
    part = part.reshape(2, 8, 1792)
    part = pick(part, z_hi) + fetch(pick(part, 1 - z_hi), "z_hi", 2, 1)
    rows = part.astype(BF16)

    line = in_order(gather(rows, Z, 8), z_hi * 4 + z_lo)
    first = jnp.stack(gather(line[:4].reshape(32, 1792), "x", 4), 0).reshape(128, 1792)
    second = jnp.stack(gather(line[4:].reshape(32, 1792), "y", 4), 0).reshape(128, 1792)
    first = jnp.stack(ring4(first, "y"))
    second = jnp.stack(ring4(second, "x"))

    both = jnp.concatenate([pair_conduction, pairs_other], 1)

    def times(a):
        return lax.dot_general(
            a.reshape(512, 1792), both, (((1,), (0,)), ((), ())), preferred_element_type=F32
        ).astype(BF16)

    first = times(first).reshape(4, 4, 4, 8, 768)
    second = times(second).reshape(4, 4, 4, 8, 768).swapaxes(0, 1)
    own = jnp.stack([first, second], 3)
    mine, theirs = own[..., :384], fetch(own[..., 384:], "core", 2, 1)
    halves = jnp.where(core == 0, jnp.stack([mine, theirs]), jnp.stack([theirs, mine]))
    halves = lax.dynamic_slice_in_dim(jnp.concatenate([halves] * 2, 1), 4 - y, 4, 1)
    halves = lax.dynamic_slice_in_dim(jnp.concatenate([halves] * 2, 2), 4 - x, 4, 2)
    return halves.transpose(1, 3, 0, 2, 4, 5, 6).reshape(2048, 384)


def solution(mesh):
    fine = Mesh(mesh.devices.reshape(4, 2, 2, 4, 4), ROW + COL)
    placed = (P(ROW, None), P(ROW, COL), P(None, ROW + COL))
    return jax.shard_map(
        per_device, mesh=fine, in_specs=placed, out_specs=P(None, ROW + COL), check_vma=False
    )
```

```python
import jax
import jax.numpy as jnp
from jax import lax
from jax.experimental import pallas as pl
from jax.experimental.pallas import tpu as pltpu
from jax.sharding import Mesh, PartitionSpec as P

ROW = ("x", "z_hi", "core")
COL = ("z_lo", "y")
Z = ("z_hi", "z_lo")
BF16 = jnp.bfloat16
F32 = jnp.float32
VMEM = pl.BlockSpec(memory_space=pltpu.VMEM)
SMEM = pl.BlockSpec(memory_space=pltpu.SMEM)
ANY = pl.BlockSpec(memory_space=pl.ANY)
HBM = pl.BlockSpec(memory_space=pltpu.HBM)
PARAMS = pltpu.CompilerParams(vmem_limit_bytes=24 * 2**20)


def fetch(block, axis, size, ahead):
    return lax.ppermute(block, axis, [((i + ahead) % size, i) for i in range(size)])


def dot_t(left, right):
    return lax.dot_general(left, right, (((0,), (0,)), ((), ())), preferred_element_type=F32)


def partial_sums(place, screening, panel, keep, send, left, right, sems):
    core = place[2]
    copies = [pltpu.make_async_copy(screening, left, sems.at[2])]
    for half, base in enumerate((1 - core, core)):
        columns = pl.ds(pl.multiple_of(base * 1024, 1024), 1024)
        copies.append(pltpu.make_async_copy(panel.at[:, columns], right.at[half], sems.at[half]))
    for copy in copies:
        copy.start()
    copies[0].wait()
    for half, out in enumerate((send, keep)):
        copies[1 + half].wait()
        for slab in range(8):
            out[slab] = dot_t(left[...], right[half, :, pl.ds(slab * 128, 128)])


def wide(block, lead):
    return jnp.concatenate([block[i].reshape(-1, 128) for i in range(lead)], 1)


def order_pairs(place, own, other, both):
    for k in range(4):
        for j in range(4):
            y, z_lo = lax.rem(place[1] + k, 4), lax.rem(place[3] + j, 4)
            rows = pl.ds(pl.multiple_of((z_lo * 4 + y) * 112, 16), 112)
            both[k, pl.ds(j * 112, 112), :384] = own[rows]
            both[k, pl.ds(j * 112, 112), 384:] = other[rows]


def product_one(one, two, both, out):
    out[0] = dot_t(wide(one, 4), both[0])
    out[1, :128] = dot_t(two[...].reshape(1792, 128), both[...].reshape(1792, 768))


def product_two(after1, before1, after2, before2, both, start, out):
    out[0] = start[0] + dot_t(wide(after1, 4), both[1]) + dot_t(wide(before1, 4), both[3])
    out[1, :128] = start[1, :128]
    for block, ahead in ((after2, 1), (before2, 3)):
        rows = pl.ds(ahead * 128, 128)
        out[1, rows] = dot_t(block[...].reshape(1792, 128), both[...].reshape(1792, 768))


def product_three(place, low1, high1, low2, high2, both, start, mine, theirs):
    x = place[0]
    for half, block in ((0, low1), (1, high1)):
        rows = pl.ds(half * 256, 256)
        total = start[0, rows] + dot_t(wide(block, 2), both[2])
        total = total.astype(BF16).reshape(2, 128, 768)
        for i in range(2):
            slab = lax.rem(x + half * 2 + i, 4)
            mine[slab, 0] = total[i, :, :384]
            theirs[slab, 0] = total[i, :, 384:]
    for ahead in (0, 1, 3):
        slab = lax.rem(x + ahead, 4)
        total = start[1, pl.ds(ahead * 128, 128)].astype(BF16)
        mine[slab, 1] = total[:, :384]
        theirs[slab, 1] = total[:, 384:]
    slab = lax.rem(x + 2, 4)
    left = jnp.concatenate([low2[...].reshape(896, 128), high2[...].reshape(896, 128)], 0)
    total = dot_t(left, both[...].reshape(1792, 768)).astype(BF16)
    mine[slab, 1] = total[:, :384]
    theirs[slab, 1] = total[:, 384:]


def place_mine(place, block, out, sem):
    rows = pl.ds(pl.multiple_of(place[2] * 1024, 1024), 1024)
    copy = pltpu.make_async_copy(block, out.at[rows], sem)
    copy.start()
    copy.wait()


def place_theirs(place, block, given, out, sem):
    rows = pl.ds(pl.multiple_of((1 - place[2]) * 1024, 1024), 1024)
    copy = pltpu.make_async_copy(block, out.at[rows], sem)
    copy.start()
    copy.wait()


def call(kernel, out_shape, operands, out_specs=VMEM, specs=None, flops=0, **more):
    return pl.pallas_call(
        kernel,
        out_shape=out_shape,
        in_specs=specs or [SMEM] + [VMEM] * (len(operands) - 1),
        out_specs=out_specs,
        compiler_params=PARAMS,
        cost_estimate=pl.CostEstimate(flops=flops, bytes_accessed=2**21, transcendentals=0),
        **more,
    )(*operands)


def per_device(pair_valence, screening, pair_conduction):
    x, y, core, z_lo = (lax.axis_index(axis) for axis in ("x", "y", "core", "z_lo"))
    place = jnp.stack([x, y, core, z_lo]).astype(jnp.int32)

    slabs = jax.ShapeDtypeStruct((8, 112, 128), F32)
    keep, send = call(
        partial_sums,
        (slabs, slabs),
        (place, screening, pair_valence),
        (VMEM, VMEM),
        [SMEM, HBM, HBM],
        scratch_shapes=[
            pltpu.VMEM((112, 112), BF16),
            pltpu.VMEM((2, 112, 1024), BF16),
            pltpu.SemaphoreType.DMA((3,)),
        ],
    )
    received, own_pairs = lax.optimization_barrier((fetch(send, "core", 2, 1), pair_conduction))
    part = (keep + received).reshape(4, 2, 112, 128)
    sent = part.astype(BF16)
    part = lax.dynamic_index_in_dim(part, x, 0, keepdims=False)
    for ahead in (1, 3, 2):
        away = lax.dynamic_index_in_dim(sent, (x + 4 - ahead) % 4, 0, keepdims=False)
        part = part + fetch(away, "x", 4, ahead).astype(F32)

    other = fetch(own_pairs, "core", 2, 1)
    both = call(
        order_pairs, jax.ShapeDtypeStruct((4, 448, 768), BF16), (place, own_pairs, other)
    )

    own = part.astype(BF16)
    up1, down1 = fetch(own, Z, 8, 1), fetch(own, Z, 8, 7)
    up1, down1, both = lax.optimization_barrier((up1, down1, both))
    up2, down2 = fetch(up1, Z, 8, 1), fetch(down1, Z, 8, 7)
    up3, down3 = fetch(up2, Z, 8, 1), fetch(down2, Z, 8, 7)
    far = jnp.concatenate([fetch(up3[:1], Z, 8, 1), fetch(down3[1:], Z, 8, 7)])
    line = [own.astype(F32) + far, up1.astype(F32) + down3, up2.astype(F32) + down2, up3.astype(F32) + down1]
    line = jnp.stack(line, 1).astype(BF16)

    def ring(block, axis):
        after, before = fetch(block, axis, 4, 1), fetch(block, axis, 4, 3)
        low, high = fetch(after[:2], axis, 4, 1), fetch(before[2:], axis, 4, 3)
        return jnp.stack([block, after, jnp.concatenate([low, high]), before])

    one, two = ring(line[0], "x"), ring(line[1], "y")
    after1, before1 = fetch(one, "y", 4, 1), fetch(one, "y", 4, 3)
    after2, before2 = fetch(two, "x", 4, 1), fetch(two, "x", 4, 3)
    total = jax.ShapeDtypeStruct((2, 512, 768), F32)
    total_one = call(product_one, total, (one, two, both), specs=[VMEM] * 3, flops=10**9)
    after1, before1, after2, before2, total_one = lax.optimization_barrier(
        (after1, before1, after2, before2, total_one)
    )
    low1, high1 = fetch(after1[:2], "y", 4, 1), fetch(before1[2:], "y", 4, 3)
    low2, high2 = fetch(after2[:2], "x", 4, 1), fetch(before2[2:], "x", 4, 3)
    total_two = call(
        product_two,
        total,
        (after1, before1, after2, before2, both, total_one),
        specs=[VMEM] * 6,
        flops=10**9,
        input_output_aliases={5: 0},
    )
    half = jax.ShapeDtypeStruct((4, 2, 128, 384), BF16)
    mine, theirs = call(
        product_three,
        (half, half),
        (place, low1, high1, low2, high2, both, total_two),
        (VMEM, VMEM),
        flops=10**9,
    )

    theirs = fetch(theirs.reshape(1024, 384), "core", 2, 1)
    out = jax.ShapeDtypeStruct((2048, 384), BF16)
    sem = dict(scratch_shapes=[pltpu.SemaphoreType.DMA])
    kernel = call(place_mine, out, (place, mine.reshape(1024, 384)), ANY, [SMEM, VMEM], **sem)
    return call(
        place_theirs,
        out,
        (place, theirs, kernel),
        ANY,
        [SMEM, VMEM, ANY],
        input_output_aliases={2: 0},
        **sem,
    )


def solution(mesh):
    fine = Mesh(mesh.devices.reshape(4, 2, 2, 4, 4), ROW + COL)
    placed = (P(ROW, None), P(ROW, COL), P(None, ROW + COL))
    return jax.shard_map(
        per_device, mesh=fine, in_specs=placed, out_specs=P(None, ROW + COL), check_vma=False
    )
```

```python
import itertools

import jax
import jax.numpy as jnp
from jax import lax
from jax.experimental import pallas as pl
from jax.experimental.pallas import tpu as pltpu
from jax.sharding import Mesh, PartitionSpec as P

ROW = ("x", "z_hi", "core")
COL = ("z_lo", "y")
Z = ("z_hi", "z_lo")
BF16 = jnp.bfloat16
F32 = jnp.float32
VMEM = pl.BlockSpec(memory_space=pltpu.VMEM)
SMEM = pl.BlockSpec(memory_space=pltpu.SMEM)
ANY = pl.BlockSpec(memory_space=pl.ANY)
PARAMS = pltpu.CompilerParams(vmem_limit_bytes=24 * 2**20)


def fetch(block, axis, size, ahead):
    return lax.ppermute(block, axis, [((i + ahead) % size, i) for i in range(size)])


def swap(block, axis, size, bits):
    return lax.ppermute(block, axis, [(i ^ bits, i) for i in range(size)])


def turn(block, order, ahead):
    pairs = []
    for x, z_hi, core, z_lo, y in itertools.product(*map(range, (4, 2, 2, 4, 4))):
        along_x = core == order
        source = ((x + ahead) % 4, y) if along_x else (x, (y + ahead) % 4)
        place = [((p * 2 + z_hi) * 2 + core) * 16 + z_lo * 4 + q for p, q in (source, (x, y))]
        pairs.append(tuple(place))
    return lax.ppermute(block, ROW + COL, pairs)


def dot_t(left, right):
    return lax.dot_general(left, right, (((0,), (0,)), ((), ())), preferred_element_type=F32)


def partial_sums(place, screening, panel, keep, send):
    core = place[2]
    for out, base in ((send, 1 - core), (keep, core)):
        for slab in range(8):
            columns = pl.ds(pl.multiple_of(base * 1024 + slab * 128, 128), 128)
            out[slab] = dot_t(screening[...], panel[:, columns])


def add_cores(place, keep, received, mine, *away):
    for back in range(4):
        for half in range(2):
            slab = lax.rem(place[0] + 4 - back, 4) * 2 + half
            total = keep[slab] + received[slab]
            if back:
                away[back - 1][half] = total.astype(BF16)
            else:
                mine[half] = total


def order_pairs(place, own, other, both):
    for k in range(4):
        for j in range(4):
            y, z_lo = lax.rem(place[1] + k, 4), place[3] ^ j
            rows = pl.ds(pl.multiple_of((z_lo * 4 + y) * 112, 16), 112)
            both[k, pl.ds(j * 112, 112), :384] = own[rows]
            both[k, pl.ds(j * 112, 112), 384:] = other[rows]


def on_core(place, core):
    return pl.when(place[2] == core)


def by_x(*slabs):
    return jnp.concatenate([slab[j].reshape(448, 128) for slab in slabs for j in range(2)], 1)


def by_y(*slabs):
    halves = [jnp.concatenate([slab[j].reshape(448, 128) for slab in slabs]) for j in range(2)]
    return jnp.concatenate(halves, 1)


def product_one(place, three, far, both, out):
    @on_core(place, 0)
    def _():
        out[:512] = dot_t(by_x(three[0], three[1]), both[0])
        out[512:] = dot_t(by_x(far, three[2]), both[0])

    @on_core(place, 1)
    def _():
        left = by_y(three[0], three[1], far, three[2])
        out[:256] = dot_t(left, both[...].reshape(1792, 768))


def product_two(place, after, after2, before, before2, both, start, out):
    @on_core(place, 0)
    def _():
        out[:512] = (
            start[:512]
            + dot_t(by_x(after[0], after[1]), both[1])
            + dot_t(by_x(before[0], before[1]), both[3])
        )
        out[512:] = (
            start[512:]
            + dot_t(by_x(after2, after[2]), both[1])
            + dot_t(by_x(before2, before[2]), both[3])
        )

    @on_core(place, 1)
    def _():
        right = both[...].reshape(1792, 768)
        out[:256] = start[:256]
        out[256:512] = dot_t(by_y(after[0], after[1], after2, after[2]), right)
        out[768:] = dot_t(by_y(before[0], before[1], before2, before[2]), right)


def product_three(place, low, both, start, mine, theirs):
    def keep(total):
        mine[...] = total[:, :384].astype(BF16)
        theirs[...] = total[:, 384:].astype(BF16)

    @on_core(place, 0)
    def _():
        keep(start[:512] + dot_t(by_x(low[0], low[1]), both[2]))

    @on_core(place, 1)
    def _():
        keep(start[:512])


def product_four(place, low, far2, far3, both, start, mine, theirs):
    def keep(rows, total):
        mine[rows] = total[:, :384].astype(BF16)
        theirs[rows] = total[:, 384:].astype(BF16)

    @on_core(place, 0)
    def _():
        keep(pl.ds(0, 512), start[512:] + dot_t(by_x(far2, far3), both[2]))

    @on_core(place, 1)
    def _():
        left = by_y(low[0], low[1], far2, far3)
        keep(pl.ds(0, 256), dot_t(left, both[...].reshape(1792, 768)))
        keep(pl.ds(256, 256), start[768:])


def place_rows(place, parts, out, sems):
    copies = []
    for block, core, first in parts:
        for i in range(2):
            row = core * 1024 + lax.rem(place[0] + first + i, 4) * 256
            rows = pl.ds(pl.multiple_of(row, 256), 256)
            sem = sems.at[len(copies)]
            copies.append(pltpu.make_async_copy(block.at[pl.ds(i * 256, 256)], out.at[rows], sem))
    for copy in copies:
        copy.start()
    for copy in copies:
        copy.wait()


def place_first(place, mine1, mine2, theirs1, out, sems):
    core = place[2]
    place_rows(place, [(mine1, core, 0), (mine2, core, 2), (theirs1, 1 - core, 0)], out, sems)


def place_last(place, theirs2, given, out, sems):
    place_rows(place, [(theirs2, 1 - place[2], 2)], out, sems)


def call(kernel, out_shape, operands, out_specs=VMEM, specs=None, flops=0, **more):
    return pl.pallas_call(
        kernel,
        out_shape=out_shape,
        in_specs=specs or [SMEM] + [VMEM] * (len(operands) - 1),
        out_specs=out_specs,
        compiler_params=PARAMS,
        cost_estimate=pl.CostEstimate(flops=flops, bytes_accessed=2**21, transcendentals=0),
        **more,
    )(*operands)


def per_device(pair_valence, screening, pair_conduction):
    x, y, core, z_lo = (lax.axis_index(axis) for axis in ("x", "y", "core", "z_lo"))
    place = jnp.stack([x, y, core, z_lo]).astype(jnp.int32)

    slabs = jax.ShapeDtypeStruct((8, 112, 128), F32)
    keep, send = call(partial_sums, (slabs, slabs), (place, screening, pair_valence), (VMEM, VMEM))
    two = jax.ShapeDtypeStruct((2, 112, 128), F32)
    sent = jax.ShapeDtypeStruct((2, 112, 128), BF16)
    part, *away = call(
        add_cores,
        (two, sent, sent, sent),
        (place, keep, fetch(send, "core", 2, 1)),
        (VMEM,) * 4,
    )
    for ahead in (1, 3, 2):
        part = part + fetch(away[ahead - 1], "x", 4, ahead).astype(F32)

    other = fetch(pair_conduction, "core", 2, 1)
    both = call(
        order_pairs, jax.ShapeDtypeStruct((4, 448, 768), BF16), (place, pair_conduction, other)
    )

    share, both = lax.optimization_barrier((swap(part.astype(BF16), "z_hi", 2, 1), both))
    part = (part + share.astype(F32)).astype(BF16)
    own = jnp.stack([part] + [swap(part, "z_lo", 4, bits) for bits in (1, 2, 3)], 1)

    after, before = turn(own, 0, 1), turn(own, 0, 3)
    three = jnp.stack([own, after, before])
    far = jnp.concatenate([turn(after[:1], 0, 1), turn(before[1:], 0, 3)])
    after, before = turn(three, 1, 1), turn(three, 1, 3)
    after2, before2 = turn(far, 1, 1), turn(far, 1, 3)
    total = jax.ShapeDtypeStruct((1024, 768), F32)
    total_one = call(product_one, total, (place, three, far, both), flops=10**9)
    after, before, total_one = lax.optimization_barrier((after, before, total_one))
    low = turn(after[:2], 1, 1)
    far3 = turn(before[2], 1, 3)
    far2 = turn(before2, 1, 3)
    total_two = call(
        product_two,
        total,
        (place, after, after2, before, before2, both, total_one),
        flops=10**9,
        input_output_aliases={6: 0},
    )
    half = jax.ShapeDtypeStruct((512, 384), BF16)
    mine1, theirs1 = call(
        product_three, (half, half), (place, low, both, total_two), (VMEM, VMEM), flops=10**9
    )
    theirs1 = fetch(theirs1, "core", 2, 1)
    mine2, theirs2 = call(
        product_four,
        (half, half),
        (place, low, far2, far3, both, total_two),
        (VMEM, VMEM),
        flops=10**9,
    )
    theirs2 = fetch(theirs2, "core", 2, 1)

    out = jax.ShapeDtypeStruct((2048, 384), BF16)
    sems = dict(scratch_shapes=[pltpu.SemaphoreType.DMA((6,))])
    kernel = call(place_first, out, (place, mine1, mine2, theirs1), ANY, **sems)
    return call(
        place_last,
        out,
        (place, theirs2, kernel),
        ANY,
        [SMEM, VMEM, ANY],
        input_output_aliases={2: 0},
        **sems,
    )


def solution(mesh):
    fine = Mesh(mesh.devices.reshape(4, 2, 2, 4, 4), ROW + COL)
    placed = (P(ROW, None), P(ROW, COL), P(None, ROW + COL))
    return jax.shard_map(
        per_device, mesh=fine, in_specs=placed, out_specs=P(None, ROW + COL), check_vma=False
    )
```

```python
import itertools

import jax
import jax.numpy as jnp
from jax import lax
from jax.experimental import pallas as pl
from jax.experimental.pallas import tpu as pltpu
from jax.sharding import Mesh, PartitionSpec as P

ROW = ("x", "z_hi", "core")
COL = ("z_lo", "y")
Z = ("z_hi", "z_lo")
ORDER = (0, 1, 3, 2)
BF16 = jnp.bfloat16
F32 = jnp.float32
VMEM = pl.BlockSpec(memory_space=pltpu.VMEM)
SMEM = pl.BlockSpec(memory_space=pltpu.SMEM)
ANY = pl.BlockSpec(memory_space=pl.ANY)
PARAMS = pltpu.CompilerParams(vmem_limit_bytes=24 * 2**20)


def fetch(block, axis, size, ahead):
    return lax.ppermute(block, axis, [((i + ahead) % size, i) for i in range(size)])


def swap(block, axis, size, bits):
    return lax.ppermute(block, axis, [(i ^ bits, i) for i in range(size)])


def turn(block, order, ahead):
    pairs = []
    for x, z_hi, core, z_lo, y in itertools.product(*map(range, (4, 2, 2, 4, 4))):
        along_x = core == order
        source = ((x + ahead) % 4, y) if along_x else (x, (y + ahead) % 4)
        place = [((p * 2 + z_hi) * 2 + core) * 16 + z_lo * 4 + q for p, q in (source, (x, y))]
        pairs.append(tuple(place))
    return lax.ppermute(block, ROW + COL, pairs)


def dot_t(left, right):
    return lax.dot_general(left, right, (((0,), (0,)), ((), ())), preferred_element_type=F32)


def partial_sums(place, screening, panel, keep, send):
    core = place[2]
    for out, base in ((send, 1 - core), (keep, core)):
        for slab in range(8):
            columns = pl.ds(pl.multiple_of(base * 1024 + slab * 128, 128), 128)
            out[slab] = dot_t(screening[...], panel[:, columns])


def add_cores(place, keep, received, mine, *away):
    for back in range(4):
        for half in range(2):
            slab = lax.rem(place[0] + 4 - back, 4) * 2 + half
            total = keep[slab] + received[slab]
            if back:
                away[back - 1][half] = total.astype(BF16)
            else:
                mine[half] = total


def order_pairs(place, own, other, both):
    for k, ahead in enumerate(ORDER):
        for j in range(4):
            y, z_lo = lax.rem(place[1] + ahead, 4), place[3] ^ j
            rows = pl.ds(pl.multiple_of((z_lo * 4 + y) * 112, 16), 112)
            both[k, pl.ds(j * 112, 112), :384] = own[rows]
            both[k, pl.ds(j * 112, 112), 384:] = other[rows]


def on_core(place, core):
    return pl.when(place[2] == core)


def by_x(*slabs):
    return jnp.concatenate([slab[j].reshape(448, 128) for slab in slabs for j in range(2)], 1)


def by_y(*slabs):
    halves = [jnp.concatenate([slab[j].reshape(448, 128) for slab in slabs]) for j in range(2)]
    return jnp.concatenate(halves, 1)


def slabs(block):
    return [block[i] for i in range(block.shape[0])]


def rows(first, count=1):
    return pl.ds(first * 256, count * 256)


def deep(both, first, count):
    return both[pl.ds(first, count)].reshape(count * 448, 768)


def product_one(place, own, after, before, both, out):
    @on_core(place, 0)
    def _():
        out[rows(0, 3)] = dot_t(by_x(own, after, before), both[0])

    @on_core(place, 1)
    def _():
        out[rows(0)] = dot_t(by_y(own, after, before), deep(both, 0, 3))


def product_two(place, far, after, before, both, start, out):
    @on_core(place, 0)
    def _():
        out[rows(0, 3)] = (
            start[rows(0, 3)] + dot_t(by_x(*slabs(after)), both[1]) + dot_t(by_x(*slabs(before)), both[2])
        )
        out[rows(3)] = dot_t(by_x(far), both[0])

    @on_core(place, 1)
    def _():
        out[rows(0)] = start[rows(0)] + dot_t(by_y(far), both[3])
        out[rows(1)] = dot_t(by_y(*slabs(after)), deep(both, 0, 3))
        out[rows(2)] = dot_t(by_y(*slabs(before)), deep(both, 0, 3))


def product_three(place, after, before, both, start, out):
    @on_core(place, 0)
    def _():
        out[rows(0, 3)] = start[rows(0, 3)]
        out[rows(3)] = start[rows(3)] + dot_t(by_x(after), both[1]) + dot_t(by_x(before), both[2])

    @on_core(place, 1)
    def _():
        out[rows(0)] = start[rows(0)]
        out[rows(1)] = start[rows(1)] + dot_t(by_y(after), both[3])
        out[rows(2)] = start[rows(2)] + dot_t(by_y(before), both[3])


def product_four(place, low, both, start, mine, theirs):
    def keep(total):
        mine[...] = total[:, :384].astype(BF16)
        theirs[...] = total[:, 384:].astype(BF16)

    @on_core(place, 0)
    def _():
        keep(start[rows(0, 2)] + dot_t(by_x(low[0], low[1]), both[3]))

    @on_core(place, 1)
    def _():
        keep(start[rows(0, 2)])


def product_five(place, low, far2, both, start, mine, theirs):
    def keep(at, total):
        mine[at] = total[:, :384].astype(BF16)
        theirs[at] = total[:, 384:].astype(BF16)

    @on_core(place, 0)
    def _():
        keep(rows(0, 2), start[rows(2, 2)] + dot_t(by_x(low[2], far2), both[3]))

    @on_core(place, 1)
    def _():
        keep(rows(0), start[rows(2)])
        keep(rows(1), dot_t(by_y(*slabs(low), far2), deep(both, 0, 4)))


def place_rows(place, parts, out, sems):
    copies = []
    for block, core, which in parts:
        for i in range(2):
            row = core * 1024 + lax.rem(place[0] + ORDER[which * 2 + i], 4) * 256
            at = pl.ds(pl.multiple_of(row, 256), 256)
            sem = sems.at[len(copies)]
            copies.append(pltpu.make_async_copy(block.at[rows(i)], out.at[at], sem))
    for copy in copies:
        copy.start()
    for copy in copies:
        copy.wait()


def place_first(place, mine1, mine2, theirs1, out, sems):
    core = place[2]
    place_rows(place, [(mine1, core, 0), (mine2, core, 1), (theirs1, 1 - core, 0)], out, sems)


def place_last(place, theirs2, given, out, sems):
    place_rows(place, [(theirs2, 1 - place[2], 1)], out, sems)


def call(kernel, out_shape, operands, out_specs=VMEM, specs=None, flops=0, **more):
    return pl.pallas_call(
        kernel,
        out_shape=out_shape,
        in_specs=specs or [SMEM] + [VMEM] * (len(operands) - 1),
        out_specs=out_specs,
        compiler_params=PARAMS,
        cost_estimate=pl.CostEstimate(flops=flops, bytes_accessed=2**21, transcendentals=0),
        **more,
    )(*operands)


def per_device(pair_valence, screening, pair_conduction):
    x, y, core, z_lo = (lax.axis_index(axis) for axis in ("x", "y", "core", "z_lo"))
    place = jnp.stack([x, y, core, z_lo]).astype(jnp.int32)

    slabs = jax.ShapeDtypeStruct((8, 112, 128), F32)
    keep, send = call(partial_sums, (slabs, slabs), (place, screening, pair_valence), (VMEM, VMEM))
    two = jax.ShapeDtypeStruct((2, 112, 128), F32)
    sent = jax.ShapeDtypeStruct((2, 112, 128), BF16)
    part, *away = call(
        add_cores,
        (two, sent, sent, sent),
        (place, keep, fetch(send, "core", 2, 1)),
        (VMEM,) * 4,
    )
    for ahead in (1, 3, 2):
        part = part + fetch(away[ahead - 1], "x", 4, ahead).astype(F32)

    other = fetch(pair_conduction, "core", 2, 1)
    both = call(
        order_pairs, jax.ShapeDtypeStruct((4, 448, 768), BF16), (place, pair_conduction, other)
    )

    share, both = lax.optimization_barrier((swap(part.astype(BF16), "z_hi", 2, 1), both))
    part = (part + share.astype(F32)).astype(BF16)
    own = jnp.stack([part] + [swap(part, "z_lo", 4, bits) for bits in (1, 2, 3)], 1)

    after, before, far = (turn(own, 0, ahead) for ahead in (1, 3, 2))
    three = [own, after, before]
    total = jax.ShapeDtypeStruct((1024, 768), F32)
    total_one = call(product_one, total, (place, *three, both), flops=10**9)
    sent = jnp.stack(three)
    after, before = turn(sent, 1, 1), turn(sent, 1, 3)
    far, total_one = lax.optimization_barrier((far, total_one))
    after2, before2 = turn(far, 1, 1), turn(far, 1, 3)
    low = turn(after, 1, 1)
    total_two = call(
        product_two,
        total,
        (place, far, after, before, both, total_one),
        flops=10**9,
        input_output_aliases={5: 0},
    )
    after2, before2, total_two = lax.optimization_barrier((after2, before2, total_two))
    far2 = turn(before2, 1, 3)
    total_three = call(
        product_three,
        total,
        (place, after2, before2, both, total_two),
        flops=10**9,
        input_output_aliases={4: 0},
    )
    half = jax.ShapeDtypeStruct((512, 384), BF16)
    mine1, theirs1 = call(
        product_four, (half, half), (place, low, both, total_three), (VMEM, VMEM), flops=10**9
    )
    theirs1 = fetch(theirs1, "core", 2, 1)
    mine2, theirs2 = call(
        product_five,
        (half, half),
        (place, low, far2, both, total_three),
        (VMEM, VMEM),
        flops=10**9,
    )
    theirs2 = fetch(theirs2, "core", 2, 1)

    out = jax.ShapeDtypeStruct((2048, 384), BF16)
    sems = dict(scratch_shapes=[pltpu.SemaphoreType.DMA((6,))])
    kernel = call(place_first, out, (place, mine1, mine2, theirs1), ANY, **sems)
    return call(
        place_last,
        out,
        (place, theirs2, kernel),
        ANY,
        [SMEM, VMEM, ANY],
        input_output_aliases={2: 0},
        **sems,
    )


def solution(mesh):
    fine = Mesh(mesh.devices.reshape(4, 2, 2, 4, 4), ROW + COL)
    placed = (P(ROW, None), P(ROW, COL), P(None, ROW + COL))
    return jax.shard_map(
        per_device, mesh=fine, in_specs=placed, out_specs=P(None, ROW + COL), check_vma=False
    )
```

```python
import itertools

import jax
import jax.numpy as jnp
from jax import lax
from jax.experimental import pallas as pl
from jax.experimental.pallas import tpu as pltpu
from jax.sharding import Mesh, PartitionSpec as P

ROW = ("x", "z_hi", "core")
COL = ("z_lo", "y")
Z = ("z_hi", "z_lo")
ORDER = (0, 1, 3, 2)
BF16 = jnp.bfloat16
F32 = jnp.float32
VMEM = pl.BlockSpec(memory_space=pltpu.VMEM)
SMEM = pl.BlockSpec(memory_space=pltpu.SMEM)
ANY = pl.BlockSpec(memory_space=pl.ANY)
PARAMS = pltpu.CompilerParams(vmem_limit_bytes=24 * 2**20)


def fetch(block, axis, size, ahead):
    return lax.ppermute(block, axis, [((i + ahead) % size, i) for i in range(size)])


def swap(block, axis, size, bits):
    return lax.ppermute(block, axis, [(i ^ bits, i) for i in range(size)])


def turn(block, order, ahead):
    pairs = []
    for x, z_hi, core, z_lo, y in itertools.product(*map(range, (4, 2, 2, 4, 4))):
        along_x = core == order
        source = ((x + ahead) % 4, y) if along_x else (x, (y + ahead) % 4)
        place = [((p * 2 + z_hi) * 2 + core) * 16 + z_lo * 4 + q for p, q in (source, (x, y))]
        pairs.append(tuple(place))
    return lax.ppermute(block, ROW + COL, pairs)


def dot_t(left, right):
    return lax.dot_general(left, right, (((0,), (0,)), ((), ())), preferred_element_type=F32)


def partial_sums(place, screening, panel, keep, send):
    core = place[2]
    for out, base in ((send, 1 - core), (keep, core)):
        for slab in range(8):
            columns = pl.ds(pl.multiple_of(base * 1024 + slab * 128, 128), 128)
            out[slab] = dot_t(screening[...], panel[:, columns])


def add_cores(place, keep, received, mine, *away):
    for back in range(4):
        for half in range(2):
            slab = lax.rem(place[0] + 4 - back, 4) * 2 + half
            total = keep[slab] + received[slab]
            if back:
                away[back - 1][half] = total.astype(BF16)
            else:
                mine[half] = total


def order_pairs(place, own, other, both):
    for k, ahead in enumerate(ORDER):
        for j in range(4):
            y, z_lo = lax.rem(place[1] + ahead, 4), place[3] ^ j
            rows = pl.ds(pl.multiple_of((z_lo * 4 + y) * 112, 16), 112)
            both[k, pl.ds(j * 112, 112), :384] = own[rows]
            both[k, pl.ds(j * 112, 112), 384:] = other[rows]


def on_core(place, core):
    return pl.when(place[2] == core)


def by_x(*slabs):
    return jnp.concatenate([slab[j].reshape(448, 128) for slab in slabs for j in range(2)], 1)


def by_y(*slabs):
    halves = [jnp.concatenate([slab[j].reshape(448, 128) for slab in slabs]) for j in range(2)]
    return jnp.concatenate(halves, 1)


def slabs(block):
    return [block.at[i] for i in range(block.shape[0])]


def rows(first, count=1):
    return pl.ds(first * 256, count * 256)


def deep(both, first, count):
    return both[pl.ds(first, count)].reshape(count * 448, 768)


def product_one(place, own, after, before, both, out):
    @on_core(place, 0)
    def _():
        out[rows(0, 3)] = dot_t(by_x(own, after, before), both[0])

    @on_core(place, 1)
    def _():
        out[rows(0)] = dot_t(by_y(own, after, before), deep(both, 0, 3))


def product_two(place, far, after, before, both, start, out):
    @on_core(place, 0)
    def _():
        out[rows(0, 3)] = (
            start[rows(0, 3)]
            + dot_t(by_x(*slabs(after)), both[1])
            + dot_t(by_x(*slabs(before)), both[2])
        )
        out[rows(3)] = dot_t(by_x(far), both[0])

    @on_core(place, 1)
    def _():
        out[rows(0)] = start[rows(0)] + dot_t(by_y(far), both[3])
        out[rows(1)] = dot_t(by_y(*slabs(after)), deep(both, 0, 3))
        out[rows(2)] = dot_t(by_y(*slabs(before)), deep(both, 0, 3))


def product_three(place, after, before, both, start, out):
    @on_core(place, 0)
    def _():
        out[rows(0, 3)] = start[rows(0, 3)]
        out[rows(3)] = start[rows(3)] + dot_t(by_x(after), both[1]) + dot_t(by_x(before), both[2])

    @on_core(place, 1)
    def _():
        out[rows(0)] = start[rows(0)]
        out[rows(1)] = start[rows(1)] + dot_t(by_y(after), both[3])
        out[rows(2)] = start[rows(2)] + dot_t(by_y(before), both[3])


def product_four(place, low, both, start, mine, theirs):
    def keep(total):
        mine[...] = total[:, :384].astype(BF16)
        theirs[...] = total[:, 384:].astype(BF16)

    @on_core(place, 0)
    def _():
        keep(start[rows(0, 2)] + dot_t(by_x(low[0], low[1]), both[3]))

    @on_core(place, 1)
    def _():
        keep(start[rows(0, 2)])


def product_five(place, low, high, both, start, mine, theirs):
    def keep(at, total):
        mine[at] = total[:, :384].astype(BF16)
        theirs[at] = total[:, 384:].astype(BF16)

    @on_core(place, 0)
    def _():
        keep(rows(0, 2), start[rows(2, 2)] + dot_t(by_x(*slabs(high)), both[3]))

    @on_core(place, 1)
    def _():
        keep(rows(0), start[rows(2)])
        keep(rows(1), dot_t(by_y(*slabs(low), *slabs(high)), deep(both, 0, 4)))


def place_rows(place, parts, out, sems):
    copies = []
    for block, core, which in parts:
        for i in range(2):
            row = core * 1024 + lax.rem(place[0] + ORDER[which * 2 + i], 4) * 256
            at = pl.ds(pl.multiple_of(row, 256), 256)
            sem = sems.at[len(copies)]
            copies.append(pltpu.make_async_copy(block.at[rows(i)], out.at[at], sem))
    for copy in copies:
        copy.start()
    for copy in copies:
        copy.wait()


def place_first(place, mine1, mine2, theirs1, out, sems):
    core = place[2]
    place_rows(place, [(mine1, core, 0), (mine2, core, 1), (theirs1, 1 - core, 0)], out, sems)


def place_last(place, theirs2, given, out, sems):
    place_rows(place, [(theirs2, 1 - place[2], 1)], out, sems)


def call(kernel, out_shape, operands, out_specs=VMEM, specs=None, **more):
    return pl.pallas_call(
        kernel,
        out_shape=out_shape,
        in_specs=specs or [SMEM] + [VMEM] * (len(operands) - 1),
        out_specs=out_specs,
        compiler_params=PARAMS,
        cost_estimate=pl.CostEstimate(flops=0, bytes_accessed=0, transcendentals=0),
        **more,
    )(*operands)


def per_device(pair_valence, screening, pair_conduction):
    x, y, core, z_lo = (lax.axis_index(axis) for axis in ("x", "y", "core", "z_lo"))
    place = jnp.stack([x, y, core, z_lo]).astype(jnp.int32)

    slabs = jax.ShapeDtypeStruct((8, 112, 128), F32)
    keep, send = call(partial_sums, (slabs, slabs), (place, screening, pair_valence), (VMEM, VMEM))
    two = jax.ShapeDtypeStruct((2, 112, 128), F32)
    sent = jax.ShapeDtypeStruct((2, 112, 128), BF16)
    part, *away = call(
        add_cores,
        (two, sent, sent, sent),
        (place, keep, fetch(send, "core", 2, 1)),
        (VMEM,) * 4,
    )
    for ahead in (1, 3, 2):
        part = part + fetch(away[ahead - 1], "x", 4, ahead).astype(F32)

    other = fetch(pair_conduction, "core", 2, 1)
    both = call(
        order_pairs, jax.ShapeDtypeStruct((4, 448, 768), BF16), (place, pair_conduction, other)
    )

    share, both = lax.optimization_barrier((swap(part.astype(BF16), "z_hi", 2, 1), both))
    part = (part + share.astype(F32)).astype(BF16)
    own = jnp.stack([part] + [swap(part, "z_lo", 4, bits) for bits in (1, 2, 3)], 1)

    after, before = turn(own, 0, 1), turn(own, 0, 3)
    far = jnp.concatenate([turn(after[:1], 0, 1), turn(before[1:], 0, 3)])
    total = jax.ShapeDtypeStruct((1024, 768), F32)
    total_one = call(product_one, total, (place, own, after, before, both))
    sent = jnp.stack([own, after, before])
    after1, before1 = turn(sent, 1, 1), turn(sent, 1, 3)
    far, total_one = lax.optimization_barrier((far, total_one))
    after2, before2 = turn(far, 1, 1), turn(far, 1, 3)
    low, high = turn(after1[:2], 1, 1), turn(jnp.stack([before1[2], before2]), 1, 3)
    total_two = call(
        product_two,
        total,
        (place, far, after1, before1, both, total_one),
        input_output_aliases={5: 0},
    )
    total_three = call(
        product_three,
        total,
        (place, after2, before2, both, total_two),
        input_output_aliases={4: 0},
    )
    half = jax.ShapeDtypeStruct((512, 384), BF16)
    mine1, theirs1 = call(
        product_four, (half, half), (place, low, both, total_three), (VMEM, VMEM)
    )
    theirs1 = fetch(theirs1, "core", 2, 1)
    mine2, theirs2 = call(
        product_five,
        (half, half),
        (place, low, high, both, total_three),
        (VMEM, VMEM),
    )
    theirs2 = fetch(theirs2, "core", 2, 1)

    out = jax.ShapeDtypeStruct((2048, 384), BF16)
    sems = dict(scratch_shapes=[pltpu.SemaphoreType.DMA((6,))])
    kernel = call(place_first, out, (place, mine1, mine2, theirs1), ANY, **sems)
    return call(
        place_last,
        out,
        (place, theirs2, kernel),
        ANY,
        [SMEM, VMEM, ANY],
        input_output_aliases={2: 0},
        **sems,
    )


def solution(mesh):
    fine = Mesh(mesh.devices.reshape(4, 2, 2, 4, 4), ROW + COL)
    placed = (P(ROW, None), P(ROW, COL), P(None, ROW + COL))
    return jax.shard_map(
        per_device, mesh=fine, in_specs=placed, out_specs=P(None, ROW + COL), check_vma=False
    )
```

```python
import itertools

import jax
import jax.numpy as jnp
from jax import lax
from jax.experimental import pallas as pl
from jax.experimental.pallas import tpu as pltpu
from jax.sharding import Mesh, PartitionSpec as P

ROW = ("x", "z_hi", "core")
COL = ("z_lo", "y")
Z = ("z_hi", "z_lo")
ORDER = (0, 1, 3, 2)
BF16 = jnp.bfloat16
F32 = jnp.float32
VMEM = pl.BlockSpec(memory_space=pltpu.VMEM)
SMEM = pl.BlockSpec(memory_space=pltpu.SMEM)
ANY = pl.BlockSpec(memory_space=pl.ANY)
PARAMS = pltpu.CompilerParams(vmem_limit_bytes=24 * 2**20)


def fetch(block, axis, size, ahead):
    return lax.ppermute(block, axis, [((i + ahead) % size, i) for i in range(size)])


def on_one(block, axis, size, source):
    if axis == "z_lo":
        pairs = [(size + source(i), size + i) for i in range(size)]
        return lax.ppermute(block, ("core", axis), pairs)
    pairs = [(source(i) * 2 + 1, i * 2 + 1) for i in range(size)]
    return lax.ppermute(block, (axis, "core"), pairs)


def turn(block, order, ahead):
    pairs = []
    for x, z_hi, core, z_lo, y in itertools.product(*map(range, (4, 2, 2, 4, 4))):
        along_x = core == order
        source = ((x + ahead) % 4, y) if along_x else (x, (y + ahead) % 4)
        place = [((p * 2 + z_hi) * 2 + core) * 16 + z_lo * 4 + q for p, q in (source, (x, y))]
        pairs.append(tuple(place))
    return lax.ppermute(block, ROW + COL, pairs)


def dot_t(left, right):
    return lax.dot_general(left, right, (((0,), (0,)), ((), ())), preferred_element_type=F32)


def partial_sums(screening, panel, keep, send):
    for slab in range(16):
        total = dot_t(screening[...], panel[:, pl.ds(slab * 128, 128)])
        keep[slab] = total
        send[slab] = total.astype(BF16)


def add_cores(place, keep, received, mine, *away):
    for back in range(4):
        for half in range(2):
            for z_hi in range(2):
                slab = half * 8 + lax.rem(place[0] + 4 - back, 4) * 2 + z_hi
                total = keep[slab] + received[slab].astype(F32)
                if back:
                    away[back - 1][half * 2 + z_hi] = total.astype(BF16)
                else:
                    mine[half * 2 + z_hi] = total


def order_pairs(place, own, other, both):
    for k, ahead in enumerate(ORDER):
        for j in range(4):
            y, z_lo = lax.rem(place[1] + ahead, 4), place[3] ^ j
            rows = pl.ds(pl.multiple_of((z_lo * 4 + y) * 112, 16), 112)
            both[k, pl.ds(j * 112, 112), :384] = own[rows]
            both[k, pl.ds(j * 112, 112), 384:] = other[rows]


def on_core(place, core):
    return pl.when(place[2] == core)


def by_x(*slabs):
    return jnp.concatenate([slab[j].reshape(448, 128) for slab in slabs for j in range(2)], 1)


def by_y(*slabs):
    halves = [jnp.concatenate([slab[j].reshape(448, 128) for slab in slabs]) for j in range(2)]
    return jnp.concatenate(halves, 1)


def slabs(block):
    return [block.at[i] for i in range(block.shape[0])]


def rows(first, count=1):
    return pl.ds(first * 256, count * 256)


def deep(both, first, count):
    return both[pl.ds(first, count)].reshape(count * 448, 768)


def product_one(place, own, after, before, both, out):
    @on_core(place, 0)
    def _():
        out[rows(0, 3)] = dot_t(by_x(own, after, before), both[0])

    @on_core(place, 1)
    def _():
        out[rows(0)] = dot_t(by_y(own, after, before), deep(both, 0, 3))


def product_two(place, far, after, before, both, start, out):
    @on_core(place, 0)
    def _():
        out[rows(0, 3)] = (
            start[rows(0, 3)]
            + dot_t(by_x(*slabs(after)), both[1])
            + dot_t(by_x(*slabs(before)), both[2])
        )
        out[rows(3)] = dot_t(by_x(far), both[0])

    @on_core(place, 1)
    def _():
        out[rows(0)] = start[rows(0)] + dot_t(by_y(far), both[3])
        out[rows(1)] = dot_t(by_y(*slabs(after)), deep(both, 0, 3))
        out[rows(2)] = dot_t(by_y(*slabs(before)), deep(both, 0, 3))


def product_three(place, after, before, both, start, out):
    @on_core(place, 0)
    def _():
        out[rows(0, 3)] = start[rows(0, 3)]
        out[rows(3)] = start[rows(3)] + dot_t(by_x(after), both[1]) + dot_t(by_x(before), both[2])

    @on_core(place, 1)
    def _():
        out[rows(0)] = start[rows(0)]
        out[rows(1)] = start[rows(1)] + dot_t(by_y(after), both[3])
        out[rows(2)] = start[rows(2)] + dot_t(by_y(before), both[3])


def product_four(place, low, both, start, mine, theirs):
    def keep(total):
        mine[...] = total[:, :384].astype(BF16)
        theirs[...] = total[:, 384:].astype(BF16)

    @on_core(place, 0)
    def _():
        keep(start[rows(0, 2)] + dot_t(by_x(low[0], low[1]), both[3]))

    @on_core(place, 1)
    def _():
        keep(start[rows(0, 2)])


def product_five(place, low, high, both, start, mine, theirs):
    def keep(at, total):
        mine[at] = total[:, :384].astype(BF16)
        theirs[at] = total[:, 384:].astype(BF16)

    @on_core(place, 0)
    def _():
        keep(rows(0, 2), start[rows(2, 2)] + dot_t(by_x(*slabs(high)), both[3]))

    @on_core(place, 1)
    def _():
        keep(rows(0), start[rows(2)])
        keep(rows(1), dot_t(by_y(*slabs(low), *slabs(high)), deep(both, 0, 4)))


def place_rows(place, parts, out, sems):
    copies = []
    for block, core, which in parts:
        for i in range(2):
            row = core * 1024 + lax.rem(place[0] + ORDER[which * 2 + i], 4) * 256
            at = pl.ds(pl.multiple_of(row, 256), 256)
            sem = sems.at[len(copies)]
            copies.append(pltpu.make_async_copy(block.at[rows(i)], out.at[at], sem))
    for copy in copies:
        copy.start()
    for copy in copies:
        copy.wait()


def place_first(place, mine1, mine2, theirs1, out, sems):
    core = place[2]
    place_rows(place, [(mine1, core, 0), (mine2, core, 1), (theirs1, 1 - core, 0)], out, sems)


def place_last(place, theirs2, given, out, sems):
    place_rows(place, [(theirs2, 1 - place[2], 1)], out, sems)


def call(kernel, out_shape, operands, out_specs=VMEM, specs=None, **more):
    return pl.pallas_call(
        kernel,
        out_shape=out_shape,
        in_specs=specs or [SMEM] + [VMEM] * (len(operands) - 1),
        out_specs=out_specs,
        compiler_params=PARAMS,
        cost_estimate=pl.CostEstimate(flops=0, bytes_accessed=0, transcendentals=0),
        **more,
    )(*operands)


def per_device(pair_valence, screening, pair_conduction):
    x, y, core, z_lo = (lax.axis_index(axis) for axis in ("x", "y", "core", "z_lo"))
    place = jnp.stack([x, y, core, z_lo]).astype(jnp.int32)

    keep, send = call(
        partial_sums,
        (jax.ShapeDtypeStruct((16, 112, 128), F32), jax.ShapeDtypeStruct((16, 112, 128), BF16)),
        (screening, pair_valence),
        (VMEM, VMEM),
        [VMEM, VMEM],
    )
    sent = jax.ShapeDtypeStruct((4, 112, 128), BF16)
    part, *away = call(
        add_cores,
        (jax.ShapeDtypeStruct((4, 112, 128), F32), sent, sent, sent),
        (place, keep, lax.ppermute(send, "core", [(0, 1)])),
        (VMEM,) * 4,
    )
    for ahead in (1, 3, 2):
        block = on_one(away[ahead - 1], "x", 4, lambda i: (i + ahead) % 4)
        part = part + block.astype(F32)

    other = fetch(pair_conduction, "core", 2, 1)
    both = call(
        order_pairs, jax.ShapeDtypeStruct((4, 448, 768), BF16), (place, pair_conduction, other)
    )

    share = on_one(part.astype(BF16), "z_hi", 2, lambda i: i ^ 1)
    share, both = lax.optimization_barrier((share, both))
    part = (part + share.astype(F32)).astype(BF16)
    line = [part] + [on_one(part, "z_lo", 4, lambda i: i ^ bits) for bits in (1, 2, 3)]
    line = jnp.stack(line, 1)
    own = jnp.where(core == 0, lax.ppermute(line[:2], "core", [(1, 0)]), line[2:])

    after, before = turn(own, 0, 1), turn(own, 0, 3)
    far = jnp.concatenate([turn(after[:1], 0, 1), turn(before[1:], 0, 3)])
    total = jax.ShapeDtypeStruct((1024, 768), F32)
    total_one = call(product_one, total, (place, own, after, before, both))
    sent = jnp.stack([own, after, before])
    after1, before1 = turn(sent, 1, 1), turn(sent, 1, 3)
    far, total_one = lax.optimization_barrier((far, total_one))
    after2, before2 = turn(far, 1, 1), turn(far, 1, 3)
    after2, before2 = lax.optimization_barrier((after2, before2))
    low, high = turn(after1[:2], 1, 1), turn(jnp.stack([before1[2], before2]), 1, 3)
    total_two = call(
        product_two,
        total,
        (place, far, after1, before1, both, total_one),
        input_output_aliases={5: 0},
    )
    total_three = call(
        product_three,
        total,
        (place, after2, before2, both, total_two),
        input_output_aliases={4: 0},
    )
    half = jax.ShapeDtypeStruct((512, 384), BF16)
    mine1, theirs1 = call(
        product_four, (half, half), (place, low, both, total_three), (VMEM, VMEM)
    )
    theirs1 = fetch(theirs1, "core", 2, 1)
    mine2, theirs2 = call(
        product_five,
        (half, half),
        (place, low, high, both, total_three),
        (VMEM, VMEM),
    )
    theirs2 = fetch(theirs2, "core", 2, 1)

    out = jax.ShapeDtypeStruct((2048, 384), BF16)
    sems = dict(scratch_shapes=[pltpu.SemaphoreType.DMA((6,))])
    kernel = call(place_first, out, (place, mine1, mine2, theirs1), ANY, **sems)
    return call(
        place_last,
        out,
        (place, theirs2, kernel),
        ANY,
        [SMEM, VMEM, ANY],
        input_output_aliases={2: 0},
        **sems,
    )


def solution(mesh):
    fine = Mesh(mesh.devices.reshape(4, 2, 2, 4, 4), ROW + COL)
    placed = (P(ROW, None), P(ROW, COL), P(None, ROW + COL))
    return jax.shard_map(
        per_device, mesh=fine, in_specs=placed, out_specs=P(None, ROW + COL), check_vma=False
    )
```

```python
import itertools

import jax
import jax.numpy as jnp
from jax import lax
from jax.experimental import pallas as pl
from jax.experimental.pallas import tpu as pltpu
from jax.sharding import Mesh, PartitionSpec as P

ROW = ("x", "z_hi", "core")
COL = ("z_lo", "y")
Z = ("z_hi", "z_lo")
ORDER = (0, 1, 3, 2)
BF16 = jnp.bfloat16
F32 = jnp.float32
VMEM = pl.BlockSpec(memory_space=pltpu.VMEM)
SMEM = pl.BlockSpec(memory_space=pltpu.SMEM)
ANY = pl.BlockSpec(memory_space=pl.ANY)
PARAMS = pltpu.CompilerParams(vmem_limit_bytes=24 * 2**20)


def fetch(block, axis, size, ahead):
    return lax.ppermute(block, axis, [((i + ahead) % size, i) for i in range(size)])


def swap(block, axis, size, bits):
    return lax.ppermute(block, axis, [(i ^ bits, i) for i in range(size)])


def turn(block, order, bits):
    pairs = []
    for x, z_hi, core, z_lo, y in itertools.product(*map(range, (4, 2, 2, 4, 4))):
        source = (x ^ bits, y) if core == order else (x, y ^ bits)
        place = [((p * 2 + z_hi) * 2 + core) * 16 + z_lo * 4 + q for p, q in (source, (x, y))]
        pairs.append(tuple(place))
    return lax.ppermute(block, ROW + COL, pairs)


def dot_t(left, right):
    return lax.dot_general(left, right, (((0,), (0,)), ((), ())), preferred_element_type=F32)


def partial_sums(place, screening, panel, keep, send):
    core = place[2]
    for out, base in ((send, 1 - core), (keep, core)):
        for slab in range(8):
            columns = pl.ds(pl.multiple_of(base * 1024 + slab * 128, 128), 128)
            out[slab] = dot_t(screening[...], panel[:, columns])


def add_cores(place, keep, received, mine, *away):
    for bits in range(4):
        for half in range(2):
            slab = (place[0] ^ bits) * 2 + half
            total = keep[slab] + received[slab]
            if bits:
                away[bits - 1][half] = total.astype(BF16)
            else:
                mine[half] = total


def order_pairs(place, own, other, both):
    for k, bits in enumerate(ORDER):
        for j in range(4):
            y, z_lo = place[1] ^ bits, place[3] ^ j
            rows = pl.ds(pl.multiple_of((z_lo * 4 + y) * 112, 16), 112)
            both[k, pl.ds(j * 112, 112), :384] = own[rows]
            both[k, pl.ds(j * 112, 112), 384:] = other[rows]


def on_core(place, core):
    return pl.when(place[2] == core)


def by_x(*slabs):
    return jnp.concatenate([slab[j].reshape(448, 128) for slab in slabs for j in range(2)], 1)


def by_y(*slabs):
    halves = [jnp.concatenate([slab[j].reshape(448, 128) for slab in slabs]) for j in range(2)]
    return jnp.concatenate(halves, 1)


def slabs(block):
    return [block.at[i] for i in range(block.shape[0])]


def rows(first, count=1):
    return pl.ds(first * 256, count * 256)


def deep(both, first, count):
    return both[pl.ds(first, count)].reshape(count * 448, 768)


def product_one(place, first, both, out):
    @on_core(place, 0)
    def _():
        out[rows(0, 2)] = dot_t(by_x(*slabs(first)), both[0])

    @on_core(place, 1)
    def _():
        out[rows(0)] = dot_t(by_y(*slabs(first)), deep(both, 0, 2))


def product_two(place, last, one, three, both, start, out):
    last, one, three = slabs(last), slabs(one), slabs(three)

    @on_core(place, 0)
    def _():
        out[rows(0, 2)] = (
            start[rows(0, 2)] + dot_t(by_x(*one), both[1]) + dot_t(by_x(*three), both[2])
        )
        out[rows(2, 2)] = dot_t(by_x(*last), both[0])

    @on_core(place, 1)
    def _():
        out[rows(0)] = start[rows(0)] + dot_t(by_y(*last), deep(both, 2, 2))
        out[rows(1)] = dot_t(by_y(*one), deep(both, 0, 2))
        out[rows(2)] = dot_t(by_y(*three), deep(both, 0, 2))


def product_three(place, one, three, both, start, out):
    one, three = slabs(one), slabs(three)

    @on_core(place, 0)
    def _():
        out[rows(0, 2)] = start[rows(0, 2)]
        out[rows(2, 2)] = (
            start[rows(2, 2)] + dot_t(by_x(*one), both[1]) + dot_t(by_x(*three), both[2])
        )

    @on_core(place, 1)
    def _():
        out[rows(0)] = start[rows(0)]
        out[rows(1)] = start[rows(1)] + dot_t(by_y(*one), deep(both, 2, 2))
        out[rows(2)] = start[rows(2)] + dot_t(by_y(*three), deep(both, 2, 2))


def product_four(place, first, both, start, mine, theirs):
    def keep(total):
        mine[...] = total[:, :384].astype(BF16)
        theirs[...] = total[:, 384:].astype(BF16)

    @on_core(place, 0)
    def _():
        keep(start[rows(0, 2)] + dot_t(by_x(*slabs(first)), both[3]))

    @on_core(place, 1)
    def _():
        keep(start[rows(0, 2)])


def product_five(place, first, last, both, start, mine, theirs):
    def keep(at, total):
        mine[at] = total[:, :384].astype(BF16)
        theirs[at] = total[:, 384:].astype(BF16)

    @on_core(place, 0)
    def _():
        keep(rows(0, 2), start[rows(2, 2)] + dot_t(by_x(*slabs(last)), both[3]))

    @on_core(place, 1)
    def _():
        keep(rows(0), start[rows(2)])
        keep(rows(1), dot_t(by_y(*slabs(first), *slabs(last)), deep(both, 0, 4)))


def place_rows(place, parts, out, sems):
    copies = []
    for block, core, which in parts:
        for i in range(2):
            row = core * 1024 + (place[0] ^ ORDER[which * 2 + i]) * 256
            at = pl.ds(pl.multiple_of(row, 256), 256)
            sem = sems.at[len(copies)]
            copies.append(pltpu.make_async_copy(block.at[rows(i)], out.at[at], sem))
    for copy in copies:
        copy.start()
    for copy in copies:
        copy.wait()


def place_first(place, mine1, mine2, theirs1, out, sems):
    core = place[2]
    place_rows(place, [(mine1, core, 0), (mine2, core, 1), (theirs1, 1 - core, 0)], out, sems)


def place_last(place, theirs2, given, out, sems):
    place_rows(place, [(theirs2, 1 - place[2], 1)], out, sems)


def call(kernel, out_shape, operands, out_specs=VMEM, specs=None, **more):
    return pl.pallas_call(
        kernel,
        out_shape=out_shape,
        in_specs=specs or [SMEM] + [VMEM] * (len(operands) - 1),
        out_specs=out_specs,
        compiler_params=PARAMS,
        cost_estimate=pl.CostEstimate(flops=0, bytes_accessed=0, transcendentals=0),
        **more,
    )(*operands)


def per_device(pair_valence, screening, pair_conduction):
    x, y, core, z_lo = (lax.axis_index(axis) for axis in ("x", "y", "core", "z_lo"))
    place = jnp.stack([x, y, core, z_lo]).astype(jnp.int32)

    slabs = jax.ShapeDtypeStruct((8, 112, 128), F32)
    keep, send = call(partial_sums, (slabs, slabs), (place, screening, pair_valence), (VMEM, VMEM))
    two = jax.ShapeDtypeStruct((2, 112, 128), F32)
    sent = jax.ShapeDtypeStruct((2, 112, 128), BF16)
    part, *away = call(
        add_cores,
        (two, sent, sent, sent),
        (place, keep, fetch(send, "core", 2, 1)),
        (VMEM,) * 4,
    )
    for bits in (1, 3, 2):
        part = part + swap(away[bits - 1], "x", 4, bits).astype(F32)

    other = fetch(pair_conduction, "core", 2, 1)
    both = call(
        order_pairs, jax.ShapeDtypeStruct((4, 448, 768), BF16), (place, pair_conduction, other)
    )

    share, both = lax.optimization_barrier((swap(part.astype(BF16), "z_hi", 2, 1), both))
    part = (part + share.astype(F32)).astype(BF16)
    own = jnp.stack([part] + [swap(part, "z_lo", 4, bits) for bits in (1, 2, 3)], 1)

    first = jnp.stack([own, turn(own, 0, 1)])
    last = turn(first, 0, 3)
    one1, three1 = turn(first, 1, 1), turn(first, 1, 3)
    total = jax.ShapeDtypeStruct((1024, 768), F32)
    total_one = call(product_one, total, (place, first, both))
    last, total_one = lax.optimization_barrier((last, total_one))
    one2, three2 = turn(last, 1, 1), turn(last, 1, 3)
    one1, three1 = lax.optimization_barrier((one1, three1))
    far1, far2 = turn(three1, 1, 1), turn(one2, 1, 3)
    total_two = call(
        product_two,
        total,
        (place, last, one1, three1, both, total_one),
        input_output_aliases={5: 0},
    )
    total_three = call(
        product_three,
        total,
        (place, one2, three2, both, total_two),
        input_output_aliases={4: 0},
    )
    half = jax.ShapeDtypeStruct((512, 384), BF16)
    mine1, theirs1 = call(
        product_four, (half, half), (place, far1, both, total_three), (VMEM, VMEM)
    )
    theirs1 = fetch(theirs1, "core", 2, 1)
    mine2, theirs2 = call(
        product_five, (half, half), (place, far1, far2, both, total_three), (VMEM, VMEM)
    )
    theirs2 = fetch(theirs2, "core", 2, 1)

    out = jax.ShapeDtypeStruct((2048, 384), BF16)
    sems = dict(scratch_shapes=[pltpu.SemaphoreType.DMA((6,))])
    kernel = call(place_first, out, (place, mine1, mine2, theirs1), ANY, **sems)
    return call(
        place_last,
        out,
        (place, theirs2, kernel),
        ANY,
        [SMEM, VMEM, ANY],
        input_output_aliases={2: 0},
        **sems,
    )


def solution(mesh):
    fine = Mesh(mesh.devices.reshape(4, 2, 2, 4, 4), ROW + COL)
    placed = (P(ROW, None), P(ROW, COL), P(None, ROW + COL))
    return jax.shard_map(
        per_device, mesh=fine, in_specs=placed, out_specs=P(None, ROW + COL), check_vma=False
    )
```

```python
import itertools

import jax
import jax.numpy as jnp
from jax import lax
from jax.experimental import pallas as pl
from jax.experimental.pallas import tpu as pltpu
from jax.sharding import Mesh, PartitionSpec as P

ROW = ("x", "z_hi", "core")
COL = ("z_lo", "y")
Z = ("z_hi", "z_lo")
ORDER = (0, 1, 3, 2)
BF16 = jnp.bfloat16
F32 = jnp.float32
VMEM = pl.BlockSpec(memory_space=pltpu.VMEM)
SMEM = pl.BlockSpec(memory_space=pltpu.SMEM)
ANY = pl.BlockSpec(memory_space=pl.ANY)
PARAMS = pltpu.CompilerParams(vmem_limit_bytes=24 * 2**20)


def fetch(block, axis, size, ahead):
    return lax.ppermute(block, axis, [((i + ahead) % size, i) for i in range(size)])


def swap(block, axis, size, bits):
    return lax.ppermute(block, axis, [(i ^ bits, i) for i in range(size)])


def turn(block, order, bits):
    pairs = []
    for x, z_hi, core, z_lo, y in itertools.product(*map(range, (4, 2, 2, 4, 4))):
        source = (x ^ bits, y) if core == order else (x, y ^ bits)
        place = [((p * 2 + z_hi) * 2 + core) * 16 + z_lo * 4 + q for p, q in (source, (x, y))]
        pairs.append(tuple(place))
    return lax.ppermute(block, ROW + COL, pairs)


def dot_t(left, right):
    return lax.dot_general(left, right, (((0,), (0,)), ((), ())), preferred_element_type=F32)


def partial_sums(place, screening, panel, keep, send):
    core = place[2]
    for out, base in ((send, 1 - core), (keep, core)):
        for slab in range(8):
            columns = pl.ds(pl.multiple_of(base * 1024 + slab * 128, 128), 128)
            out[slab] = dot_t(screening[...], panel[:, columns])


def add_cores(place, keep, received, mine, *away):
    for bits in range(4):
        for half in range(2):
            slab = (place[0] ^ bits) * 2 + half
            total = keep[slab] + received[slab]
            if bits:
                away[bits - 1][half] = total.astype(BF16)
            else:
                mine[half] = total


def order_pairs(place, own, other, both):
    for k, bits in enumerate(ORDER):
        for j in range(4):
            y, z_lo = place[1] ^ bits, place[3] ^ j
            rows = pl.ds(pl.multiple_of((z_lo * 4 + y) * 112, 16), 112)
            both[k, pl.ds(j * 112, 112), :384] = own[rows]
            both[k, pl.ds(j * 112, 112), 384:] = other[rows]


def on_core(place, core):
    return pl.when(place[2] == core)


def by_x(*slabs):
    return jnp.concatenate([slab[j].reshape(448, 128) for slab in slabs for j in range(2)], 1)


def by_y(*slabs):
    halves = [jnp.concatenate([slab[j].reshape(448, 128) for slab in slabs]) for j in range(2)]
    return jnp.concatenate(halves, 1)


def slabs(block):
    return [block.at[i] for i in range(block.shape[0])]


def rows(first, count=1):
    return pl.ds(first * 256, count * 256)


def deep(both, first, count):
    return both[pl.ds(first, count)].reshape(count * 448, 768)


def product_one(place, first, both, out):
    @on_core(place, 0)
    def _():
        out[rows(0, 2)] = dot_t(by_x(*slabs(first)), both[0])

    @on_core(place, 1)
    def _():
        out[rows(0)] = dot_t(by_y(*slabs(first)), deep(both, 0, 2))


def product_two(place, last, one, three, both, start, out):
    last, one, three = slabs(last), slabs(one), slabs(three)

    @on_core(place, 0)
    def _():
        out[rows(0, 2)] = (
            start[rows(0, 2)] + dot_t(by_x(*one), both[1]) + dot_t(by_x(*three), both[2])
        )
        out[rows(2, 2)] = dot_t(by_x(*last), both[0])

    @on_core(place, 1)
    def _():
        out[rows(0)] = start[rows(0)] + dot_t(by_y(*last), deep(both, 2, 2))
        out[rows(1)] = dot_t(by_y(*one), deep(both, 0, 2))
        out[rows(2)] = dot_t(by_y(*three), deep(both, 0, 2))


def product_three(place, one, three, both, start, out):
    one, three = slabs(one), slabs(three)

    @on_core(place, 0)
    def _():
        out[rows(0, 2)] = start[rows(0, 2)]
        out[rows(2, 2)] = (
            start[rows(2, 2)] + dot_t(by_x(*one), both[1]) + dot_t(by_x(*three), both[2])
        )

    @on_core(place, 1)
    def _():
        out[rows(0)] = start[rows(0)]
        out[rows(1)] = start[rows(1)] + dot_t(by_y(*one), deep(both, 2, 2))
        out[rows(2)] = start[rows(2)] + dot_t(by_y(*three), deep(both, 2, 2))


def product_four(place, first, both, start, mine, theirs):
    def keep(total):
        mine[...] = total[:, :384].astype(BF16)
        theirs[...] = total[:, 384:].astype(BF16)

    @on_core(place, 0)
    def _():
        keep(start[rows(0, 2)] + dot_t(by_x(*slabs(first)), both[3]))

    @on_core(place, 1)
    def _():
        keep(start[rows(0, 2)])


def product_five(place, first, last, both, start, mine, theirs):
    def keep(at, total):
        mine[at] = total[:, :384].astype(BF16)
        theirs[at] = total[:, 384:].astype(BF16)

    @on_core(place, 0)
    def _():
        keep(rows(0, 2), start[rows(2, 2)] + dot_t(by_x(*slabs(last)), both[3]))

    @on_core(place, 1)
    def _():
        keep(rows(0), start[rows(2)])
        keep(rows(1), dot_t(by_y(*slabs(first), *slabs(last)), deep(both, 0, 4)))


def place_rows(place, parts, out, sems):
    copies = []
    for block, core, which in parts:
        for i in range(2):
            row = core * 1024 + (place[0] ^ ORDER[which * 2 + i]) * 256
            at = pl.ds(pl.multiple_of(row, 256), 256)
            sem = sems.at[len(copies)]
            copies.append(pltpu.make_async_copy(block.at[rows(i)], out.at[at], sem))
    for copy in copies:
        copy.start()
    for copy in copies:
        copy.wait()


def place_first(place, mine1, mine2, theirs1, out, sems):
    core = place[2]
    place_rows(place, [(mine1, core, 0), (mine2, core, 1), (theirs1, 1 - core, 0)], out, sems)


def place_last(place, theirs2, given, out, sems):
    place_rows(place, [(theirs2, 1 - place[2], 1)], out, sems)


def call(kernel, out_shape, operands, out_specs=VMEM, specs=None, **more):
    return pl.pallas_call(
        kernel,
        out_shape=out_shape,
        in_specs=specs or [SMEM] + [VMEM] * (len(operands) - 1),
        out_specs=out_specs,
        compiler_params=PARAMS,
        cost_estimate=pl.CostEstimate(flops=0, bytes_accessed=0, transcendentals=0),
        **more,
    )(*operands)


def per_device(pair_valence, screening, pair_conduction):
    x, y, core, z_lo = (lax.axis_index(axis) for axis in ("x", "y", "core", "z_lo"))
    place = jnp.stack([x, y, core, z_lo]).astype(jnp.int32)

    slabs = jax.ShapeDtypeStruct((8, 112, 128), F32)
    keep, send = call(partial_sums, (slabs, slabs), (place, screening, pair_valence), (VMEM, VMEM))
    two = jax.ShapeDtypeStruct((2, 112, 128), F32)
    sent = jax.ShapeDtypeStruct((2, 112, 128), BF16)
    part, *away = call(
        add_cores,
        (two, sent, sent, sent),
        (place, keep, fetch(send, "core", 2, 1)),
        (VMEM,) * 4,
    )
    for bits in (1, 3, 2):
        part = part + swap(away[bits - 1], "x", 4, bits).astype(F32)

    other = fetch(pair_conduction, "core", 2, 1)
    both = call(
        order_pairs, jax.ShapeDtypeStruct((4, 448, 768), BF16), (place, pair_conduction, other)
    )

    share, both = lax.optimization_barrier((swap(part.astype(BF16), "z_hi", 2, 1), both))
    part = (part + share.astype(F32)).astype(BF16)
    own = jnp.stack([part] + [swap(part, "z_lo", 4, bits) for bits in (1, 2, 3)], 1)

    first = jnp.stack([own, turn(own, 0, 1)])
    last = turn(first, 0, 3)
    total = jax.ShapeDtypeStruct((1024, 768), F32)
    total_one = call(product_one, total, (place, first, both))
    first, total_one = lax.optimization_barrier((first, total_one))
    one1 = turn(first, 1, 1)
    first, last, one1 = lax.optimization_barrier((first, last, one1))
    three1, one2, three2 = turn(first, 1, 3), turn(last, 1, 1), turn(last, 1, 3)
    far1, far2 = turn(three1, 1, 1), turn(one2, 1, 3)
    total_two = call(
        product_two,
        total,
        (place, last, one1, three1, both, total_one),
        input_output_aliases={5: 0},
    )
    total_three = call(
        product_three,
        total,
        (place, one2, three2, both, total_two),
        input_output_aliases={4: 0},
    )
    half = jax.ShapeDtypeStruct((512, 384), BF16)
    mine1, theirs1 = call(
        product_four, (half, half), (place, far1, both, total_three), (VMEM, VMEM)
    )
    theirs1 = fetch(theirs1, "core", 2, 1)
    mine2, theirs2 = call(
        product_five, (half, half), (place, far1, far2, both, total_three), (VMEM, VMEM)
    )
    theirs2 = fetch(theirs2, "core", 2, 1)

    out = jax.ShapeDtypeStruct((2048, 384), BF16)
    sems = dict(scratch_shapes=[pltpu.SemaphoreType.DMA((6,))])
    kernel = call(place_first, out, (place, mine1, mine2, theirs1), ANY, **sems)
    return call(
        place_last,
        out,
        (place, theirs2, kernel),
        ANY,
        [SMEM, VMEM, ANY],
        input_output_aliases={2: 0},
        **sems,
    )


def solution(mesh):
    fine = Mesh(mesh.devices.reshape(4, 2, 2, 4, 4), ROW + COL)
    placed = (P(ROW, None), P(ROW, COL), P(None, ROW + COL))
    return jax.shard_map(
        per_device, mesh=fine, in_specs=placed, out_specs=P(None, ROW + COL), check_vma=False
    )
```

```python
import functools
import itertools

import jax
import jax.numpy as jnp
from jax import lax
from jax.experimental import pallas as pl
from jax.experimental.pallas import tpu as pltpu
from jax.sharding import Mesh, PartitionSpec as P

ROW = ("x", "z_hi", "core")
COL = ("z_lo", "y")
Z = ("z_hi", "z_lo")
ORDER = (0, 1, 3, 2)
BF16 = jnp.bfloat16
F32 = jnp.float32
VMEM = pl.BlockSpec(memory_space=pltpu.VMEM)
SMEM = pl.BlockSpec(memory_space=pltpu.SMEM)
ANY = pl.BlockSpec(memory_space=pl.ANY)
PARAMS = pltpu.CompilerParams(vmem_limit_bytes=24 * 2**20)


def fetch(block, axis, size, ahead):
    return lax.ppermute(block, axis, [((i + ahead) % size, i) for i in range(size)])


def swap(block, axis, size, bits):
    return lax.ppermute(block, axis, [(i ^ bits, i) for i in range(size)])


def turn(block, order, bits):
    pairs = []
    for x, z_hi, core, z_lo, y in itertools.product(*map(range, (4, 2, 2, 4, 4))):
        source = (x ^ bits, y) if core == order else (x, y ^ bits)
        place = [((p * 2 + z_hi) * 2 + core) * 16 + z_lo * 4 + q for p, q in (source, (x, y))]
        pairs.append(tuple(place))
    return lax.ppermute(block, ROW + COL, pairs)


def dot_t(left, right):
    return lax.dot_general(left, right, (((0,), (0,)), ((), ())), preferred_element_type=F32)


def partial_sums(place, screening, panel, keep, send):
    core = place[2]
    for out, base in ((send, 1 - core), (keep, core)):
        for slab in range(8):
            columns = pl.ds(pl.multiple_of(base * 1024 + slab * 128, 128), 128)
            out[slab] = dot_t(screening[...], panel[:, columns])


def add_cores(place, keep, received, mine, *away):
    for bits in range(4):
        for half in range(2):
            slab = (place[0] ^ bits) * 2 + half
            total = keep[slab] + received[slab]
            if bits:
                away[bits - 1][half] = total.astype(BF16)
            else:
                mine[half] = total


def order_pairs(place, own, other, both):
    for k, bits in enumerate(ORDER):
        for j in range(4):
            y, z_lo = place[1] ^ bits, place[3] ^ j
            rows = pl.ds(pl.multiple_of((z_lo * 4 + y) * 112, 16), 112)
            both[k, pl.ds(j * 112, 112), :384] = own[rows]
            both[k, pl.ds(j * 112, 112), 384:] = other[rows]


def on_core(place, core):
    return pl.when(place[2] == core)


def by_x(*slabs):
    return jnp.concatenate([slab[j].reshape(448, 128) for slab in slabs for j in range(2)], 1)


def by_y(*slabs):
    halves = [jnp.concatenate([slab[j].reshape(448, 128) for slab in slabs]) for j in range(2)]
    return jnp.concatenate(halves, 1)


def slabs(block):
    return [block.at[i] for i in range(block.shape[0])]


def rows(first, count=1):
    return pl.ds(first * 256, count * 256)


def deep(both, first, count):
    return both[pl.ds(first, count)].reshape(count * 448, 768)


def product_one(place, first, both, out):
    @on_core(place, 0)
    def _():
        out[rows(0, 2)] = dot_t(by_x(*slabs(first)), both[0])

    @on_core(place, 1)
    def _():
        out[rows(0)] = dot_t(by_y(*slabs(first)), deep(both, 0, 2))


def product_two(place, last, one, three, both, start, out):
    last, one, three = slabs(last), slabs(one), slabs(three)

    @on_core(place, 0)
    def _():
        out[rows(0, 2)] = (
            start[rows(0, 2)] + dot_t(by_x(*one), both[1]) + dot_t(by_x(*three), both[2])
        )
        out[rows(2, 2)] = dot_t(by_x(*last), both[0])

    @on_core(place, 1)
    def _():
        out[rows(0)] = start[rows(0)] + dot_t(by_y(*last), deep(both, 2, 2))
        out[rows(1)] = dot_t(by_y(*one), deep(both, 0, 2))
        out[rows(2)] = dot_t(by_y(*three), deep(both, 0, 2))


def product_three(place, one, three, both, start, out):
    one, three = slabs(one), slabs(three)

    @on_core(place, 0)
    def _():
        out[rows(0, 2)] = start[rows(0, 2)]
        out[rows(2, 2)] = (
            start[rows(2, 2)] + dot_t(by_x(*one), both[1]) + dot_t(by_x(*three), both[2])
        )

    @on_core(place, 1)
    def _():
        out[rows(0)] = start[rows(0)]
        out[rows(1)] = start[rows(1)] + dot_t(by_y(*one), deep(both, 2, 2))
        out[rows(2)] = start[rows(2)] + dot_t(by_y(*three), deep(both, 2, 2))


def product_four(place, first, both, start, mine, theirs):
    def keep(total):
        mine[...] = total[:, :384].astype(BF16)
        theirs[...] = total[:, 384:].astype(BF16)

    @on_core(place, 0)
    def _():
        keep(start[rows(0, 2)] + dot_t(by_x(*slabs(first)), both[3]))

    @on_core(place, 1)
    def _():
        keep(start[rows(0, 2)])


def product_five(side, place, first, last, both, start, out):
    columns = pl.ds(side * 384, 384)

    @on_core(place, 0)
    def _():
        total = start[rows(2, 2), columns] + dot_t(by_x(*slabs(last)), both[3, :, columns])
        out[...] = total.astype(BF16)

    @on_core(place, 1)
    def _():
        out[rows(0)] = start[rows(2), columns].astype(BF16)
        left = by_y(*slabs(first), *slabs(last))
        out[rows(1)] = dot_t(left, both[:, :, columns].reshape(1792, 384)).astype(BF16)


def place_rows(place, parts, out, sems):
    copies = []
    for block, core, which in parts:
        for i in range(2):
            row = core * 1024 + (place[0] ^ ORDER[which * 2 + i]) * 256
            at = pl.ds(pl.multiple_of(row, 256), 256)
            sem = sems.at[len(copies)]
            copies.append(pltpu.make_async_copy(block.at[rows(i)], out.at[at], sem))
    for copy in copies:
        copy.start()
    for copy in copies:
        copy.wait()


def place_first(place, mine1, mine2, theirs1, out, sems):
    core = place[2]
    place_rows(place, [(mine1, core, 0), (mine2, core, 1), (theirs1, 1 - core, 0)], out, sems)


def place_last(place, theirs2, given, out, sems):
    place_rows(place, [(theirs2, 1 - place[2], 1)], out, sems)


def call(kernel, out_shape, operands, out_specs=VMEM, specs=None, **more):
    return pl.pallas_call(
        kernel,
        out_shape=out_shape,
        in_specs=specs or [SMEM] + [VMEM] * (len(operands) - 1),
        out_specs=out_specs,
        compiler_params=PARAMS,
        cost_estimate=pl.CostEstimate(flops=0, bytes_accessed=0, transcendentals=0),
        **more,
    )(*operands)


def per_device(pair_valence, screening, pair_conduction):
    x, y, core, z_lo = (lax.axis_index(axis) for axis in ("x", "y", "core", "z_lo"))
    place = jnp.stack([x, y, core, z_lo]).astype(jnp.int32)

    slabs = jax.ShapeDtypeStruct((8, 112, 128), F32)
    keep, send = call(partial_sums, (slabs, slabs), (place, screening, pair_valence), (VMEM, VMEM))
    two = jax.ShapeDtypeStruct((2, 112, 128), F32)
    sent = jax.ShapeDtypeStruct((2, 112, 128), BF16)
    part, *away = call(
        add_cores,
        (two, sent, sent, sent),
        (place, keep, fetch(send, "core", 2, 1)),
        (VMEM,) * 4,
    )
    for bits in (1, 3, 2):
        part = part + swap(away[bits - 1], "x", 4, bits).astype(F32)

    other = fetch(pair_conduction, "core", 2, 1)
    both = call(
        order_pairs, jax.ShapeDtypeStruct((4, 448, 768), BF16), (place, pair_conduction, other)
    )

    share, both = lax.optimization_barrier((swap(part.astype(BF16), "z_hi", 2, 1), both))
    part = (part + share.astype(F32)).astype(BF16)
    own = jnp.stack([part] + [swap(part, "z_lo", 4, bits) for bits in (1, 2, 3)], 1)

    near1, near3 = turn(own, 0, 1), turn(own, 0, 3)
    far = turn(near1, 0, 3)
    first = jnp.stack([own, near1])
    total = jax.ShapeDtypeStruct((1024, 768), F32)
    total_one = call(product_one, total, (place, first, both))
    first, total_one = lax.optimization_barrier((first, total_one))
    one1, three1 = turn(first, 1, 1), turn(first, 1, 3)
    last = jnp.stack([near3, far])
    one2, three2 = turn(last, 1, 1), turn(last, 1, 3)
    one1, three1 = lax.optimization_barrier((one1, three1))
    far1, far2 = turn(three1, 1, 1), turn(one2, 1, 3)
    total_two = call(
        product_two,
        total,
        (place, last, one1, three1, both, total_one),
        input_output_aliases={5: 0},
    )
    total_three = call(
        product_three,
        total,
        (place, one2, three2, both, total_two),
        input_output_aliases={4: 0},
    )
    half = jax.ShapeDtypeStruct((512, 384), BF16)
    mine1, theirs1 = call(
        product_four, (half, half), (place, far1, both, total_three), (VMEM, VMEM)
    )
    theirs1 = fetch(theirs1, "core", 2, 1)
    mine2, theirs2 = (
        call(functools.partial(product_five, side), half, (place, far1, far2, both, total_three))
        for side in (0, 1)
    )
    theirs2 = fetch(theirs2, "core", 2, 1)

    out = jax.ShapeDtypeStruct((2048, 384), BF16)
    sems = dict(scratch_shapes=[pltpu.SemaphoreType.DMA((6,))])
    kernel = call(place_first, out, (place, mine1, mine2, theirs1), ANY, **sems)
    return call(
        place_last,
        out,
        (place, theirs2, kernel),
        ANY,
        [SMEM, VMEM, ANY],
        input_output_aliases={2: 0},
        **sems,
    )


def solution(mesh):
    fine = Mesh(mesh.devices.reshape(4, 2, 2, 4, 4), ROW + COL)
    placed = (P(ROW, None), P(ROW, COL), P(None, ROW + COL))
    return jax.shard_map(
        per_device, mesh=fine, in_specs=placed, out_specs=P(None, ROW + COL), check_vma=False
    )
```

```python
import functools
import itertools

import jax
import jax.numpy as jnp
from jax import lax
from jax.experimental import pallas as pl
from jax.experimental.pallas import tpu as pltpu
from jax.sharding import Mesh, PartitionSpec as P

ROW = ("x", "z_hi", "core")
COL = ("z_lo", "y")
Z = ("z_hi", "z_lo")
ORDER = (0, 1, 3, 2)
BF16 = jnp.bfloat16
F32 = jnp.float32
VMEM = pl.BlockSpec(memory_space=pltpu.VMEM)
SMEM = pl.BlockSpec(memory_space=pltpu.SMEM)
ANY = pl.BlockSpec(memory_space=pl.ANY)
PARAMS = pltpu.CompilerParams(vmem_limit_bytes=24 * 2**20)


def fetch(block, axis, size, ahead):
    return lax.ppermute(block, axis, [((i + ahead) % size, i) for i in range(size)])


def swap(block, axis, size, bits):
    return lax.ppermute(block, axis, [(i ^ bits, i) for i in range(size)])


def turn(block, order, bits):
    pairs = []
    for x, z_hi, core, z_lo, y in itertools.product(*map(range, (4, 2, 2, 4, 4))):
        source = (x ^ bits, y) if core == order else (x, y ^ bits)
        place = [((p * 2 + z_hi) * 2 + core) * 16 + z_lo * 4 + q for p, q in (source, (x, y))]
        pairs.append(tuple(place))
    return lax.ppermute(block, ROW + COL, pairs)


def dot_t(left, right):
    return lax.dot_general(left, right, (((0,), (0,)), ((), ())), preferred_element_type=F32)


def partial_sums(place, screening, panel, keep, send):
    core = place[2]
    for out, base in ((send, 1 - core), (keep, core)):
        for slab in range(8):
            columns = pl.ds(pl.multiple_of(base * 1024 + slab * 128, 128), 128)
            out[slab] = dot_t(screening[...], panel[:, columns])


def add_cores(place, keep, received, mine, *away):
    for bits in range(4):
        for half in range(2):
            slab = (place[0] ^ bits) * 2 + half
            total = keep[slab] + received[slab]
            if bits:
                away[bits - 1][half] = total.astype(BF16)
            else:
                mine[half] = total


def order_pairs(place, own, other, both):
    for k, bits in enumerate(ORDER):
        for j in range(4):
            y, z_lo = place[1] ^ bits, place[3] ^ j
            rows = pl.ds(pl.multiple_of((z_lo * 4 + y) * 112, 16), 112)
            both[k, pl.ds(j * 112, 112), :384] = own[rows]
            both[k, pl.ds(j * 112, 112), 384:] = other[rows]


def on_core(place, core):
    return pl.when(place[2] == core)


def by_x(*slabs):
    return jnp.concatenate([slab[j].reshape(448, 128) for slab in slabs for j in range(2)], 1)


def by_y(*slabs):
    halves = [jnp.concatenate([slab[j].reshape(448, 128) for slab in slabs]) for j in range(2)]
    return jnp.concatenate(halves, 1)


def rows(first, count=1):
    return pl.ds(first * 256, count * 256)


def deep(both, first, count):
    return both[pl.ds(first, count)].reshape(count * 448, 768)


def product_one(place, own, near1, both, out):
    @on_core(place, 0)
    def _():
        out[rows(0, 2)] = dot_t(by_x(own, near1), both[0])

    @on_core(place, 1)
    def _():
        out[rows(0)] = dot_t(by_y(own, near1), deep(both, 0, 2))


def product_two(place, near3, far, own1, near1, own3, near31, both, start, out):
    @on_core(place, 0)
    def _():
        out[rows(0, 2)] = (
            start[rows(0, 2)]
            + dot_t(by_x(own1, near1), both[1])
            + dot_t(by_x(own3, near31), both[2])
        )
        out[rows(2, 2)] = dot_t(by_x(near3, far), both[0])

    @on_core(place, 1)
    def _():
        out[rows(0)] = start[rows(0)] + dot_t(by_y(near3, far), deep(both, 2, 2))
        out[rows(1)] = dot_t(by_y(own1, near1), deep(both, 0, 2))
        out[rows(2)] = dot_t(by_y(own3, near31), deep(both, 0, 2))


def product_three(place, near1, far1, near3, far3, both, start, out):
    @on_core(place, 0)
    def _():
        out[rows(0, 2)] = start[rows(0, 2)]
        out[rows(2, 2)] = (
            start[rows(2, 2)]
            + dot_t(by_x(near1, far1), both[1])
            + dot_t(by_x(near3, far3), both[2])
        )

    @on_core(place, 1)
    def _():
        out[rows(0)] = start[rows(0)]
        out[rows(1)] = start[rows(1)] + dot_t(by_y(near1, far1), deep(both, 2, 2))
        out[rows(2)] = start[rows(2)] + dot_t(by_y(near3, far3), deep(both, 2, 2))


def product_four(place, own, near1, both, start, mine, theirs):
    def keep(total):
        mine[...] = total[:, :384].astype(BF16)
        theirs[...] = total[:, 384:].astype(BF16)

    @on_core(place, 0)
    def _():
        keep(start[rows(0, 2)] + dot_t(by_x(own, near1), both[3]))

    @on_core(place, 1)
    def _():
        keep(start[rows(0, 2)])


def product_five(side, place, own, near1, near3, far, both, start, out):
    columns = pl.ds(side * 384, 384)

    @on_core(place, 0)
    def _():
        total = start[rows(2, 2), columns] + dot_t(by_x(near3, far), both[3, :, columns])
        out[...] = total.astype(BF16)

    @on_core(place, 1)
    def _():
        out[rows(0)] = start[rows(2), columns].astype(BF16)
        left = by_y(own, near1, near3, far)
        out[rows(1)] = dot_t(left, both[:, :, columns].reshape(1792, 384)).astype(BF16)


def place_rows(place, parts, out, sems):
    copies = []
    for block, core, which in parts:
        for i in range(2):
            row = core * 1024 + (place[0] ^ ORDER[which * 2 + i]) * 256
            at = pl.ds(pl.multiple_of(row, 256), 256)
            sem = sems.at[len(copies)]
            copies.append(pltpu.make_async_copy(block.at[rows(i)], out.at[at], sem))
    for copy in copies:
        copy.start()
    for copy in copies:
        copy.wait()


def place_first(place, mine1, mine2, theirs1, out, sems):
    core = place[2]
    place_rows(place, [(mine1, core, 0), (mine2, core, 1), (theirs1, 1 - core, 0)], out, sems)


def place_last(place, theirs2, given, out, sems):
    place_rows(place, [(theirs2, 1 - place[2], 1)], out, sems)


def call(kernel, out_shape, operands, out_specs=VMEM, specs=None, **more):
    return pl.pallas_call(
        kernel,
        out_shape=out_shape,
        in_specs=specs or [SMEM] + [VMEM] * (len(operands) - 1),
        out_specs=out_specs,
        compiler_params=PARAMS,
        cost_estimate=pl.CostEstimate(flops=0, bytes_accessed=0, transcendentals=0),
        **more,
    )(*operands)


def per_device(pair_valence, screening, pair_conduction):
    x, y, core, z_lo = (lax.axis_index(axis) for axis in ("x", "y", "core", "z_lo"))
    place = jnp.stack([x, y, core, z_lo]).astype(jnp.int32)

    slabs = jax.ShapeDtypeStruct((8, 112, 128), F32)
    keep, send = call(partial_sums, (slabs, slabs), (place, screening, pair_valence), (VMEM, VMEM))
    two = jax.ShapeDtypeStruct((2, 112, 128), F32)
    sent = jax.ShapeDtypeStruct((2, 112, 128), BF16)
    part, *away = call(
        add_cores,
        (two, sent, sent, sent),
        (place, keep, fetch(send, "core", 2, 1)),
        (VMEM,) * 4,
    )
    for bits in (3, 2, 1):
        part = part + swap(away[bits - 1], "x", 4, bits).astype(F32)

    other = fetch(pair_conduction, "core", 2, 1)
    both = call(
        order_pairs, jax.ShapeDtypeStruct((4, 448, 768), BF16), (place, pair_conduction, other)
    )

    share, both = lax.optimization_barrier((swap(part.astype(BF16), "z_hi", 2, 1), both))
    part = (part + share.astype(F32)).astype(BF16)
    own = jnp.stack([part] + [swap(part, "z_lo", 4, bits) for bits in (1, 2, 3)], 1)

    near1, near3 = turn(own, 0, 1), turn(own, 0, 3)
    far = turn(near1, 0, 3)
    one_own, three_own = turn(own, 1, 1), turn(own, 1, 3)
    total = jax.ShapeDtypeStruct((1024, 768), F32)
    total_one = call(product_one, total, (place, own, near1, both))
    one_near1, three_near1 = turn(near1, 1, 1), turn(near1, 1, 3)
    one_near3, three_near3 = turn(near3, 1, 1), turn(near3, 1, 3)
    one_far, three_far = turn(far, 1, 1), turn(far, 1, 3)
    far_own, far_near1 = turn(three_own, 1, 1), turn(three_near1, 1, 1)
    far_near3, far_far = turn(one_near3, 1, 3), turn(one_far, 1, 3)
    total_two = call(
        product_two,
        total,
        (place, near3, far, one_own, one_near1, three_own, three_near1, both, total_one),
        input_output_aliases={8: 0},
    )
    total_three = call(
        product_three,
        total,
        (place, one_near3, one_far, three_near3, three_far, both, total_two),
        input_output_aliases={6: 0},
    )
    half = jax.ShapeDtypeStruct((512, 384), BF16)
    mine1, theirs1 = call(
        product_four, (half, half), (place, far_own, far_near1, both, total_three), (VMEM, VMEM)
    )
    theirs1 = fetch(theirs1, "core", 2, 1)
    mine2, theirs2 = (
        call(
            functools.partial(product_five, side),
            half,
            (place, far_own, far_near1, far_near3, far_far, both, total_three),
        )
        for side in (0, 1)
    )
    theirs2 = fetch(theirs2, "core", 2, 1)

    out = jax.ShapeDtypeStruct((2048, 384), BF16)
    sems = dict(scratch_shapes=[pltpu.SemaphoreType.DMA((6,))])
    kernel = call(place_first, out, (place, mine1, mine2, theirs1), ANY, **sems)
    return call(
        place_last,
        out,
        (place, theirs2, kernel),
        ANY,
        [SMEM, VMEM, ANY],
        input_output_aliases={2: 0},
        **sems,
    )


def solution(mesh):
    fine = Mesh(mesh.devices.reshape(4, 2, 2, 4, 4), ROW + COL)
    placed = (P(ROW, None), P(ROW, COL), P(None, ROW + COL))
    return jax.shard_map(
        per_device, mesh=fine, in_specs=placed, out_specs=P(None, ROW + COL), check_vma=False
    )
```

```python
import functools
import itertools

import jax
import jax.numpy as jnp
from jax import lax
from jax.experimental import pallas as pl
from jax.experimental.pallas import tpu as pltpu
from jax.sharding import Mesh, PartitionSpec as P

ROW = ("x", "z_hi", "core")
COL = ("z_lo", "y")
Z = ("z_hi", "z_lo")
ORDER = (0, 1, 3, 2)
BF16 = jnp.bfloat16
F32 = jnp.float32
VMEM = pl.BlockSpec(memory_space=pltpu.VMEM)
SMEM = pl.BlockSpec(memory_space=pltpu.SMEM)
ANY = pl.BlockSpec(memory_space=pl.ANY)
PARAMS = pltpu.CompilerParams(vmem_limit_bytes=24 * 2**20)


def fetch(block, axis, size, ahead):
    return lax.ppermute(block, axis, [((i + ahead) % size, i) for i in range(size)])


def swap(block, axis, size, bits):
    return lax.ppermute(block, axis, [(i ^ bits, i) for i in range(size)])


def turn(block, order, bits):
    pairs = []
    for x, z_hi, core, z_lo, y in itertools.product(*map(range, (4, 2, 2, 4, 4))):
        source = (x ^ bits, y) if core == order else (x, y ^ bits)
        place = [((p * 2 + z_hi) * 2 + core) * 16 + z_lo * 4 + q for p, q in (source, (x, y))]
        pairs.append(tuple(place))
    return lax.ppermute(block, ROW + COL, pairs)


def dot_t(left, right):
    return lax.dot_general(left, right, (((0,), (0,)), ((), ())), preferred_element_type=F32)


def partial_sums(place, screening, panel, keep, send):
    core = place[2]
    for out, base in ((send, 1 - core), (keep, core)):
        for slab in range(8):
            columns = pl.ds(pl.multiple_of(base * 1024 + slab * 128, 128), 128)
            out[slab] = dot_t(screening[...], panel[:, columns])


def add_cores(place, keep, received, mine, *away):
    for bits in range(4):
        for half in range(2):
            slab = (place[0] ^ bits) * 2 + half
            total = keep[slab] + received[slab]
            if bits:
                away[bits - 1][half] = total.astype(BF16)
            else:
                mine[half] = total


def order_pairs(place, own, other, both):
    for k, bits in enumerate(ORDER):
        for j in range(4):
            y, z_lo = place[1] ^ bits, place[3] ^ j
            rows = pl.ds(pl.multiple_of((z_lo * 4 + y) * 112, 16), 112)
            both[k, pl.ds(j * 112, 112), :384] = own[rows]
            both[k, pl.ds(j * 112, 112), 384:] = other[rows]


def on_core(place, core):
    return pl.when(place[2] == core)


def by_x(*slabs):
    return jnp.concatenate([slab[j].reshape(448, 128) for slab in slabs for j in range(2)], 1)


def by_y(*slabs):
    halves = [jnp.concatenate([slab[j].reshape(448, 128) for slab in slabs]) for j in range(2)]
    return jnp.concatenate(halves, 1)


def rows(first, count=1):
    return pl.ds(first * 256, count * 256)


def deep(both, first, count):
    return both[pl.ds(first, count)].reshape(count * 448, 768)


def product_one(place, own, near1, both, low):
    @on_core(place, 0)
    def _():
        low[...] = dot_t(by_x(own, near1), both[0])

    @on_core(place, 1)
    def _():
        low[rows(0)] = dot_t(by_y(own, near1), deep(both, 0, 2))


def product_two(place, near3, far, own1, near1, own3, near31, both, start, low, high):
    @on_core(place, 0)
    def _():
        low[...] = (
            start[...] + dot_t(by_x(own1, near1), both[1]) + dot_t(by_x(own3, near31), both[2])
        )
        high[...] = dot_t(by_x(near3, far), both[0])

    @on_core(place, 1)
    def _():
        low[rows(0)] = start[rows(0)] + dot_t(by_y(near3, far), deep(both, 2, 2))
        low[rows(1)] = dot_t(by_y(own1, near1), deep(both, 0, 2))
        high[rows(0)] = dot_t(by_y(own3, near31), deep(both, 0, 2))


def product_three(place, near31, far1, own, near1, both, low, mine, theirs):
    def keep(at, total):
        mine[at] = total[:, :384].astype(BF16)
        theirs[at] = total[:, 384:].astype(BF16)

    @on_core(place, 0)
    def _():
        keep(rows(0, 2), low[...] + dot_t(by_x(own, near1), both[3]))

    @on_core(place, 1)
    def _():
        keep(rows(0), low[rows(0)])
        keep(rows(1), low[rows(1)] + dot_t(by_y(near31, far1), deep(both, 2, 2)))


def product_four(place, near31, far1, near33, far3, both, start, high):
    @on_core(place, 0)
    def _():
        high[...] = (
            start[...] + dot_t(by_x(near31, far1), both[1]) + dot_t(by_x(near33, far3), both[2])
        )

    @on_core(place, 1)
    def _():
        high[rows(0)] = start[rows(0)] + dot_t(by_y(near33, far3), deep(both, 2, 2))


def product_five(side, place, own, near1, near3, far, both, high, out):
    columns = pl.ds(side * 384, 384)

    @on_core(place, 0)
    def _():
        total = high[:, columns] + dot_t(by_x(near3, far), both[3, :, columns])
        out[...] = total.astype(BF16)

    @on_core(place, 1)
    def _():
        out[rows(0)] = high[rows(0), columns].astype(BF16)
        left = by_y(own, near1, near3, far)
        out[rows(1)] = dot_t(left, both[:, :, columns].reshape(1792, 384)).astype(BF16)


def place_rows(place, mine1, mine2, theirs1, theirs2, out, sems):
    copies = []
    for block, core, which in (
        (mine1, place[2], 0),
        (mine2, place[2], 1),
        (theirs1, 1 - place[2], 0),
        (theirs2, 1 - place[2], 1),
    ):
        for i in range(2):
            row = core * 1024 + (place[0] ^ ORDER[which * 2 + i]) * 256
            at = pl.ds(pl.multiple_of(row, 256), 256)
            sem = sems.at[len(copies)]
            copies.append(pltpu.make_async_copy(block.at[rows(i)], out.at[at], sem))
    for copy in copies:
        copy.start()
    for copy in copies:
        copy.wait()


def call(kernel, out_shape, operands, out_specs=VMEM, specs=None, **more):
    return pl.pallas_call(
        kernel,
        out_shape=out_shape,
        in_specs=specs or [SMEM] + [VMEM] * (len(operands) - 1),
        out_specs=out_specs,
        compiler_params=PARAMS,
        cost_estimate=pl.CostEstimate(flops=0, bytes_accessed=0, transcendentals=0),
        **more,
    )(*operands)


def per_device(pair_valence, screening, pair_conduction):
    x, y, core, z_lo = (lax.axis_index(axis) for axis in ("x", "y", "core", "z_lo"))
    place = jnp.stack([x, y, core, z_lo]).astype(jnp.int32)

    slabs = jax.ShapeDtypeStruct((8, 112, 128), F32)
    keep, send = call(partial_sums, (slabs, slabs), (place, screening, pair_valence), (VMEM, VMEM))
    two = jax.ShapeDtypeStruct((2, 112, 128), F32)
    sent = jax.ShapeDtypeStruct((2, 112, 128), BF16)
    part, *away = call(
        add_cores,
        (two, sent, sent, sent),
        (place, keep, fetch(send, "core", 2, 1)),
        (VMEM,) * 4,
    )
    for bits in (3, 2, 1):
        part = part + swap(away[bits - 1], "x", 4, bits).astype(F32)

    other = fetch(pair_conduction, "core", 2, 1)
    both = call(
        order_pairs, jax.ShapeDtypeStruct((4, 448, 768), BF16), (place, pair_conduction, other)
    )

    share, both = lax.optimization_barrier((swap(part.astype(BF16), "z_hi", 2, 1), both))
    part = (part + share.astype(F32)).astype(BF16)
    own = jnp.stack([part] + [swap(part, "z_lo", 4, bits) for bits in (1, 2, 3)], 1)

    near1, near3 = turn(own, 0, 1), turn(own, 0, 3)
    far = turn(near1, 0, 3)
    one_own, three_own = turn(own, 1, 1), turn(own, 1, 3)
    total = jax.ShapeDtypeStruct((512, 768), F32)
    low = call(product_one, total, (place, own, near1, both))
    one_near1, three_near1 = turn(near1, 1, 1), turn(near1, 1, 3)
    one_near3, three_near3 = turn(near3, 1, 1), turn(near3, 1, 3)
    one_far, three_far = turn(far, 1, 1), turn(far, 1, 3)
    far_own, far_near1 = turn(three_own, 1, 1), turn(three_near1, 1, 1)
    far_near3, far_far = turn(one_near3, 1, 3), turn(one_far, 1, 3)
    low, high = call(
        product_two,
        (total, total),
        (place, near3, far, one_own, one_near1, three_own, three_near1, both, low),
        (VMEM, VMEM),
    )
    half = jax.ShapeDtypeStruct((512, 384), BF16)
    low, three_near3, three_far = lax.optimization_barrier((low, three_near3, three_far))
    mine1, theirs1 = call(
        product_three,
        (half, half),
        (place, one_near3, one_far, far_own, far_near1, both, low),
        (VMEM, VMEM),
    )
    theirs1 = fetch(theirs1, "core", 2, 1)
    high = call(
        product_four,
        total,
        (place, one_near3, one_far, three_near3, three_far, both, high),
    )
    mine2, theirs2 = (
        call(
            functools.partial(product_five, side),
            half,
            (place, far_own, far_near1, far_near3, far_far, both, high),
        )
        for side in (0, 1)
    )
    theirs2 = fetch(theirs2, "core", 2, 1)
    return call(
        place_rows,
        jax.ShapeDtypeStruct((2048, 384), BF16),
        (place, mine1, mine2, theirs1, theirs2),
        ANY,
        scratch_shapes=[pltpu.SemaphoreType.DMA((8,))],
    )


def solution(mesh):
    fine = Mesh(mesh.devices.reshape(4, 2, 2, 4, 4), ROW + COL)
    placed = (P(ROW, None), P(ROW, COL), P(None, ROW + COL))
    return jax.shard_map(
        per_device, mesh=fine, in_specs=placed, out_specs=P(None, ROW + COL), check_vma=False
    )
```

```python
import functools
import itertools

import jax
import jax.numpy as jnp
from jax import lax
from jax.experimental import pallas as pl
from jax.experimental.pallas import tpu as pltpu
from jax.sharding import Mesh, PartitionSpec as P

ROW = ("x", "z_hi", "core")
COL = ("z_lo", "y")
Z = ("z_hi", "z_lo")
ORDER = (0, 1, 3, 2)
BF16 = jnp.bfloat16
F32 = jnp.float32
VMEM = pl.BlockSpec(memory_space=pltpu.VMEM)
SMEM = pl.BlockSpec(memory_space=pltpu.SMEM)
ANY = pl.BlockSpec(memory_space=pl.ANY)
PARAMS = pltpu.CompilerParams(vmem_limit_bytes=24 * 2**20)


def fetch(block, axis, size, ahead):
    return lax.ppermute(block, axis, [((i + ahead) % size, i) for i in range(size)])


def swap(block, axis, size, bits):
    return lax.ppermute(block, axis, [(i ^ bits, i) for i in range(size)])


def turn(block, order, bits):
    pairs = []
    for x, z_hi, core, z_lo, y in itertools.product(*map(range, (4, 2, 2, 4, 4))):
        source = (x ^ bits, y) if core == order else (x, y ^ bits)
        place = [((p * 2 + z_hi) * 2 + core) * 16 + z_lo * 4 + q for p, q in (source, (x, y))]
        pairs.append(tuple(place))
    return lax.ppermute(block, ROW + COL, pairs)


def dot_t(left, right):
    return lax.dot_general(left, right, (((0,), (0,)), ((), ())), preferred_element_type=F32)


def partial_sums(place, screening, panel, keep, send):
    core = place[2]
    for out, base in ((send, 1 - core), (keep, core)):
        for slab in range(8):
            columns = pl.ds(pl.multiple_of(base * 1024 + slab * 128, 128), 128)
            out[slab] = dot_t(screening[...], panel[:, columns])


def add_cores(place, keep, received, mine, *away):
    for bits in range(4):
        for half in range(2):
            slab = (place[0] ^ bits) * 2 + half
            total = keep[slab] + received[slab]
            if bits:
                away[bits - 1][half] = total.astype(BF16)
            else:
                mine[half] = total


def order_pairs(place, own, other, both):
    for k, bits in enumerate(ORDER):
        for j in range(4):
            y, z_lo = place[1] ^ bits, place[3] ^ j
            rows = pl.ds(pl.multiple_of((z_lo * 4 + y) * 112, 16), 112)
            both[k, pl.ds(j * 112, 112), :384] = own[rows]
            both[k, pl.ds(j * 112, 112), 384:] = other[rows]


def on_core(place, core):
    return pl.when(place[2] == core)


def by_x(*slabs):
    return jnp.concatenate([slab[j].reshape(448, 128) for slab in slabs for j in range(2)], 1)


def by_y(*slabs):
    halves = [jnp.concatenate([slab[j].reshape(448, 128) for slab in slabs]) for j in range(2)]
    return jnp.concatenate(halves, 1)


def rows(first, count=1):
    return pl.ds(first * 256, count * 256)


def deep(both, first, count):
    return both[pl.ds(first, count)].reshape(count * 448, 768)


def product_one(place, own, both, out):
    @on_core(place, 0)
    def _():
        out[...] = dot_t(by_x(own), both[0])

    @on_core(place, 1)
    def _():
        out[...] = dot_t(by_y(own), both[0])


def product_two(place, near1, near3, far, own1, near11, own3, near31, both, start, low, high):
    @on_core(place, 0)
    def _():
        total = dot_t(by_x(own1, near11), both[1]) + dot_t(by_x(own3, near31), both[2])
        low[rows(0)] = start[...] + total[:256]
        low[rows(1)] = dot_t(by_x(near1), both[0]) + total[256:]
        high[...] = dot_t(by_x(near3, far), both[0])

    @on_core(place, 1)
    def _():
        low[rows(0)] = start[...] + dot_t(by_y(near1, near3, far), deep(both, 1, 3))
        low[rows(1)] = dot_t(by_y(own1, near11), deep(both, 0, 2))
        high[rows(0)] = dot_t(by_y(own3, near31), deep(both, 0, 2))


def product_three(place, near31, far1, own, near1, both, low, mine, theirs):
    def keep(at, total):
        mine[at] = total[:, :384].astype(BF16)
        theirs[at] = total[:, 384:].astype(BF16)

    @on_core(place, 0)
    def _():
        keep(rows(0, 2), low[...] + dot_t(by_x(own, near1), both[3]))

    @on_core(place, 1)
    def _():
        keep(rows(0), low[rows(0)])
        keep(rows(1), low[rows(1)] + dot_t(by_y(near31, far1), deep(both, 2, 2)))


def product_four(place, near31, far1, near33, far3, both, start, high):
    @on_core(place, 0)
    def _():
        high[...] = (
            start[...] + dot_t(by_x(near31, far1), both[1]) + dot_t(by_x(near33, far3), both[2])
        )

    @on_core(place, 1)
    def _():
        high[rows(0)] = start[rows(0)] + dot_t(by_y(near33, far3), deep(both, 2, 2))


def product_five(side, place, own, near1, near3, far, both, high, out):
    columns = pl.ds(side * 384, 384)

    @on_core(place, 0)
    def _():
        total = high[:, columns] + dot_t(by_x(near3, far), both[3, :, columns])
        out[...] = total.astype(BF16)

    @on_core(place, 1)
    def _():
        out[rows(0)] = high[rows(0), columns].astype(BF16)
        left = by_y(own, near1, near3, far)
        out[rows(1)] = dot_t(left, both[:, :, columns].reshape(1792, 384)).astype(BF16)


def place_rows(place, mine1, mine2, theirs1, theirs2, out, sems):
    copies = []
    for block, core, which in (
        (mine1, place[2], 0),
        (mine2, place[2], 1),
        (theirs1, 1 - place[2], 0),
        (theirs2, 1 - place[2], 1),
    ):
        for i in range(2):
            row = core * 1024 + (place[0] ^ ORDER[which * 2 + i]) * 256
            at = pl.ds(pl.multiple_of(row, 256), 256)
            sem = sems.at[len(copies)]
            copies.append(pltpu.make_async_copy(block.at[rows(i)], out.at[at], sem))
    for copy in copies:
        copy.start()
    for copy in copies:
        copy.wait()


def call(kernel, out_shape, operands, out_specs=VMEM, specs=None, **more):
    return pl.pallas_call(
        kernel,
        out_shape=out_shape,
        in_specs=specs or [SMEM] + [VMEM] * (len(operands) - 1),
        out_specs=out_specs,
        compiler_params=PARAMS,
        cost_estimate=pl.CostEstimate(flops=0, bytes_accessed=0, transcendentals=0),
        **more,
    )(*operands)


def per_device(pair_valence, screening, pair_conduction):
    x, y, core, z_lo = (lax.axis_index(axis) for axis in ("x", "y", "core", "z_lo"))
    place = jnp.stack([x, y, core, z_lo]).astype(jnp.int32)

    slabs = jax.ShapeDtypeStruct((8, 112, 128), F32)
    keep, send = call(partial_sums, (slabs, slabs), (place, screening, pair_valence), (VMEM, VMEM))
    two = jax.ShapeDtypeStruct((2, 112, 128), F32)
    sent = jax.ShapeDtypeStruct((2, 112, 128), BF16)
    part, *away = call(
        add_cores,
        (two, sent, sent, sent),
        (place, keep, fetch(send, "core", 2, 1)),
        (VMEM,) * 4,
    )
    for bits in (3, 2, 1):
        part = part + swap(away[bits - 1], "x", 4, bits).astype(F32)

    other = fetch(pair_conduction, "core", 2, 1)
    both = call(
        order_pairs, jax.ShapeDtypeStruct((4, 448, 768), BF16), (place, pair_conduction, other)
    )

    share, both = lax.optimization_barrier((swap(part.astype(BF16), "z_hi", 2, 1), both))
    part = (part + share.astype(F32)).astype(BF16)
    own = jnp.stack([part] + [swap(part, "z_lo", 4, bits) for bits in (1, 2, 3)], 1)

    near1, near3 = turn(own, 0, 1), turn(own, 0, 3)
    total = jax.ShapeDtypeStruct((512, 768), F32)
    start = call(product_one, jax.ShapeDtypeStruct((256, 768), F32), (place, own, both))
    near1, start = lax.optimization_barrier((near1, start))
    far = turn(near1, 0, 3)
    one_own, three_own = turn(own, 1, 1), turn(own, 1, 3)
    one_near1, three_near1 = turn(near1, 1, 1), turn(near1, 1, 3)
    near3, one_own = lax.optimization_barrier((near3, one_own))
    one_near3, three_near3 = turn(near3, 1, 1), turn(near3, 1, 3)
    one_far, three_far = turn(far, 1, 1), turn(far, 1, 3)
    far_own, far_near1 = turn(three_own, 1, 1), turn(three_near1, 1, 1)
    far_near3, far_far = turn(one_near3, 1, 3), turn(one_far, 1, 3)
    low, high = call(
        product_two,
        (total, total),
        (place, near1, near3, far, one_own, one_near1, three_own, three_near1, both, start),
        (VMEM, VMEM),
    )
    half = jax.ShapeDtypeStruct((512, 384), BF16)
    low, three_near3, three_far = lax.optimization_barrier((low, three_near3, three_far))
    mine1, theirs1 = call(
        product_three,
        (half, half),
        (place, one_near3, one_far, far_own, far_near1, both, low),
        (VMEM, VMEM),
    )
    theirs1 = fetch(theirs1, "core", 2, 1)
    high = call(
        product_four,
        total,
        (place, one_near3, one_far, three_near3, three_far, both, high),
    )
    mine2, theirs2 = (
        call(
            functools.partial(product_five, side),
            half,
            (place, far_own, far_near1, far_near3, far_far, both, high),
        )
        for side in (0, 1)
    )
    theirs2 = fetch(theirs2, "core", 2, 1)
    return call(
        place_rows,
        jax.ShapeDtypeStruct((2048, 384), BF16),
        (place, mine1, mine2, theirs1, theirs2),
        ANY,
        scratch_shapes=[pltpu.SemaphoreType.DMA((8,))],
    )


def solution(mesh):
    fine = Mesh(mesh.devices.reshape(4, 2, 2, 4, 4), ROW + COL)
    placed = (P(ROW, None), P(ROW, COL), P(None, ROW + COL))
    return jax.shard_map(
        per_device, mesh=fine, in_specs=placed, out_specs=P(None, ROW + COL), check_vma=False
    )
```

```python
import functools
import itertools

import jax
import jax.numpy as jnp
from jax import lax
from jax.experimental import pallas as pl
from jax.experimental.pallas import tpu as pltpu
from jax.sharding import Mesh, PartitionSpec as P

ROW = ("x", "z_hi", "core")
COL = ("z_lo", "y")
Z = ("z_hi", "z_lo")
ORDER = (0, 1, 3, 2)
BF16 = jnp.bfloat16
F32 = jnp.float32
VMEM = pl.BlockSpec(memory_space=pltpu.VMEM)
SMEM = pl.BlockSpec(memory_space=pltpu.SMEM)
ANY = pl.BlockSpec(memory_space=pl.ANY)
PARAMS = pltpu.CompilerParams(vmem_limit_bytes=24 * 2**20)


def fetch(block, axis, size, ahead):
    return lax.ppermute(block, axis, [((i + ahead) % size, i) for i in range(size)])


def swap(block, axis, size, bits):
    return lax.ppermute(block, axis, [(i ^ bits, i) for i in range(size)])


def turn(block, order, bits):
    pairs = []
    for x, z_hi, core, z_lo, y in itertools.product(*map(range, (4, 2, 2, 4, 4))):
        source = (x ^ bits, y) if core == order else (x, y ^ bits)
        place = [((p * 2 + z_hi) * 2 + core) * 16 + z_lo * 4 + q for p, q in (source, (x, y))]
        pairs.append(tuple(place))
    return lax.ppermute(block, ROW + COL, pairs)


def dot_t(left, right):
    return lax.dot_general(left, right, (((0,), (0,)), ((), ())), preferred_element_type=F32)


def partial_sums(place, screening, panel, keep, send):
    core = place[2]
    for out, base in ((send, 1 - core), (keep, core)):
        for slab in range(8):
            columns = pl.ds(pl.multiple_of(base * 1024 + slab * 128, 128), 128)
            out[slab] = dot_t(screening[...], panel[:, columns])


def add_cores(place, keep, received, mine, *away):
    for bits in range(4):
        for half in range(2):
            slab = (place[0] ^ bits) * 2 + half
            total = keep[slab] + received[slab]
            if bits:
                away[bits - 1][half] = total.astype(BF16)
            else:
                mine[half] = total


def order_pairs(place, own, other, both):
    for k, bits in enumerate(ORDER):
        for j in range(4):
            y, z_lo = place[1] ^ bits, place[3] ^ j
            rows = pl.ds(pl.multiple_of((z_lo * 4 + y) * 112, 16), 112)
            both[k, pl.ds(j * 112, 112), :384] = own[rows]
            both[k, pl.ds(j * 112, 112), 384:] = other[rows]


def on_core(place, core):
    return pl.when(place[2] == core)


def by_x(*slabs):
    return jnp.concatenate([slab[j].reshape(448, 128) for slab in slabs for j in range(2)], 1)


def by_y(*slabs):
    halves = [jnp.concatenate([slab[j].reshape(448, 128) for slab in slabs]) for j in range(2)]
    return jnp.concatenate(halves, 1)


def rows(first, count=1):
    return pl.ds(first * 256, count * 256)


def deep(both, first, count):
    return both[pl.ds(first, count)].reshape(count * 448, 768)


def product_one(place, own, both, out):
    @on_core(place, 0)
    def _():
        out[...] = dot_t(by_x(own), both[0])

    @on_core(place, 1)
    def _():
        out[...] = dot_t(by_y(own), both[0])


def product_two(place, near1, near3, far, own1, near11, own3, near31, both, start, low, high):
    @on_core(place, 0)
    def _():
        total = dot_t(by_x(own1, near11), both[1]) + dot_t(by_x(own3, near31), both[2])
        low[rows(0)] = start[...] + total[:256]
        low[rows(1)] = dot_t(by_x(near1), both[0]) + total[256:]
        high[...] = dot_t(by_x(near3, far), both[0])

    @on_core(place, 1)
    def _():
        low[rows(0)] = start[...] + dot_t(by_y(near1, near3, far), deep(both, 1, 3))
        low[rows(1)] = dot_t(by_y(own1, near11), deep(both, 0, 2))
        high[rows(0)] = dot_t(by_y(own3, near31), deep(both, 0, 2))


def product_three(place, near31, far1, own, near1, both, low, mine, theirs):
    def keep(at, total):
        mine[at] = total[:, :384].astype(BF16)
        theirs[at] = total[:, 384:].astype(BF16)

    @on_core(place, 0)
    def _():
        keep(rows(0, 2), low[...] + dot_t(by_x(own, near1), both[3]))

    @on_core(place, 1)
    def _():
        keep(rows(0), low[rows(0)])
        keep(rows(1), low[rows(1)] + dot_t(by_y(near31, far1), deep(both, 2, 2)))


def product_four(place, near31, far1, near33, far3, both, start, high):
    @on_core(place, 0)
    def _():
        high[...] = (
            start[...] + dot_t(by_x(near31, far1), both[1]) + dot_t(by_x(near33, far3), both[2])
        )

    @on_core(place, 1)
    def _():
        high[rows(0)] = start[rows(0)] + dot_t(by_y(near33, far3), deep(both, 2, 2))


def product_five(side, place, own, near1, near3, far, both, high, out):
    columns = pl.ds(side * 384, 384)

    @on_core(place, 0)
    def _():
        total = high[:, columns] + dot_t(by_x(near3, far), both[3, :, columns])
        out[...] = total.astype(BF16)

    @on_core(place, 1)
    def _():
        out[rows(0)] = high[rows(0), columns].astype(BF16)
        left = by_y(own, near1, near3, far)
        out[rows(1)] = dot_t(left, both[:, :, columns].reshape(1792, 384)).astype(BF16)


def place_rows(place, mine1, mine2, theirs1, theirs2, out, sems):
    copies = []
    for block, core, which in (
        (mine1, place[2], 0),
        (mine2, place[2], 1),
        (theirs1, 1 - place[2], 0),
        (theirs2, 1 - place[2], 1),
    ):
        for i in range(2):
            row = core * 1024 + (place[0] ^ ORDER[which * 2 + i]) * 256
            at = pl.ds(pl.multiple_of(row, 256), 256)
            sem = sems.at[len(copies)]
            copies.append(pltpu.make_async_copy(block.at[rows(i)], out.at[at], sem))
    for copy in copies:
        copy.start()
    for copy in copies:
        copy.wait()


def call(kernel, out_shape, operands, out_specs=VMEM, specs=None, **more):
    return pl.pallas_call(
        kernel,
        out_shape=out_shape,
        in_specs=specs or [SMEM] + [VMEM] * (len(operands) - 1),
        out_specs=out_specs,
        compiler_params=PARAMS,
        cost_estimate=pl.CostEstimate(flops=0, bytes_accessed=0, transcendentals=0),
        **more,
    )(*operands)


def per_device(pair_valence, screening, pair_conduction):
    x, y, core, z_lo = (lax.axis_index(axis) for axis in ("x", "y", "core", "z_lo"))
    place = jnp.stack([x, y, core, z_lo]).astype(jnp.int32)

    slabs = jax.ShapeDtypeStruct((8, 112, 128), F32)
    keep, send = call(partial_sums, (slabs, slabs), (place, screening, pair_valence), (VMEM, VMEM))
    two = jax.ShapeDtypeStruct((2, 112, 128), F32)
    sent = jax.ShapeDtypeStruct((2, 112, 128), BF16)
    part, *away = call(
        add_cores,
        (two, sent, sent, sent),
        (place, keep, fetch(send, "core", 2, 1)),
        (VMEM,) * 4,
    )
    for bits in (3, 2, 1):
        part = part + swap(away[bits - 1], "x", 4, bits).astype(F32)

    other = fetch(pair_conduction, "core", 2, 1)
    both = call(
        order_pairs, jax.ShapeDtypeStruct((4, 448, 768), BF16), (place, pair_conduction, other)
    )

    share, both = lax.optimization_barrier((swap(part.astype(BF16), "z_hi", 2, 1), both))
    part = (part + share.astype(F32)).astype(BF16)
    own = jnp.stack([part] + [swap(part, "z_lo", 4, bits) for bits in (1, 2, 3)], 1)

    near1, near3 = turn(own, 0, 1), turn(own, 0, 3)
    total = jax.ShapeDtypeStruct((512, 768), F32)
    start = call(product_one, jax.ShapeDtypeStruct((256, 768), F32), (place, own, both))
    near1, start = lax.optimization_barrier((near1, start))
    far = turn(near1, 0, 3)
    one_own, three_own = turn(own, 1, 1), turn(own, 1, 3)
    one_near1, three_near1 = turn(near1, 1, 1), turn(near1, 1, 3)
    near3, one_own = lax.optimization_barrier((near3, one_own))
    one_near3, three_near3 = turn(near3, 1, 1), turn(near3, 1, 3)
    one_far, three_far = turn(far, 1, 1), turn(far, 1, 3)
    far_own, far_near1 = turn(three_own, 1, 1), turn(three_near1, 1, 1)
    far_near3, far_far = turn(one_near3, 1, 3), turn(one_far, 1, 3)
    low, high = call(
        product_two,
        (total, total),
        (place, near1, near3, far, one_own, one_near1, three_own, three_near1, both, start),
        (VMEM, VMEM),
    )
    high = call(
        product_four,
        total,
        (place, one_near3, one_far, three_near3, three_far, both, high),
    )
    far_near1, high = lax.optimization_barrier((far_near1, high))
    half = jax.ShapeDtypeStruct((512, 384), BF16)
    mine1, theirs1 = call(
        product_three,
        (half, half),
        (place, one_near3, one_far, far_own, far_near1, both, low),
        (VMEM, VMEM),
    )
    theirs1 = fetch(theirs1, "core", 2, 1)
    mine2, theirs2 = (
        call(
            functools.partial(product_five, side),
            half,
            (place, far_own, far_near1, far_near3, far_far, both, high),
        )
        for side in (0, 1)
    )
    theirs2 = fetch(theirs2, "core", 2, 1)
    return call(
        place_rows,
        jax.ShapeDtypeStruct((2048, 384), BF16),
        (place, mine1, mine2, theirs1, theirs2),
        ANY,
        scratch_shapes=[pltpu.SemaphoreType.DMA((8,))],
    )


def solution(mesh):
    fine = Mesh(mesh.devices.reshape(4, 2, 2, 4, 4), ROW + COL)
    placed = (P(ROW, None), P(ROW, COL), P(None, ROW + COL))
    return jax.shard_map(
        per_device, mesh=fine, in_specs=placed, out_specs=P(None, ROW + COL), check_vma=False
    )
```

```python
import functools
import itertools

import jax
import jax.numpy as jnp
from jax import lax
from jax.experimental import pallas as pl
from jax.experimental.pallas import tpu as pltpu
from jax.sharding import Mesh, PartitionSpec as P

ROW = ("x", "z_hi", "core")
COL = ("z_lo", "y")
Z = ("z_hi", "z_lo")
ORDER = (0, 1, 3, 2)
BF16 = jnp.bfloat16
F32 = jnp.float32
VMEM = pl.BlockSpec(memory_space=pltpu.VMEM)
SMEM = pl.BlockSpec(memory_space=pltpu.SMEM)
ANY = pl.BlockSpec(memory_space=pl.ANY)
PARAMS = pltpu.CompilerParams(vmem_limit_bytes=24 * 2**20)


def fetch(block, axis, size, ahead):
    return lax.ppermute(block, axis, [((i + ahead) % size, i) for i in range(size)])


def swap(block, axis, size, bits):
    return lax.ppermute(block, axis, [(i ^ bits, i) for i in range(size)])


def turn(block, order, bits):
    pairs = []
    for x, z_hi, core, z_lo, y in itertools.product(*map(range, (4, 2, 2, 4, 4))):
        source = (x ^ bits, y) if core == order else (x, y ^ bits)
        place = [((p * 2 + z_hi) * 2 + core) * 16 + z_lo * 4 + q for p, q in (source, (x, y))]
        pairs.append(tuple(place))
    return lax.ppermute(block, ROW + COL, pairs)


def dot_t(left, right):
    return lax.dot_general(left, right, (((0,), (0,)), ((), ())), preferred_element_type=F32)


def partial_sums(place, screening, panel, keep, send):
    core = place[2]
    for out, base in ((send, 1 - core), (keep, core)):
        for slab in range(8):
            columns = pl.ds(pl.multiple_of(base * 1024 + slab * 128, 128), 128)
            out[slab] = dot_t(screening[...].astype(BF16), panel[:, columns])


def add_cores(place, keep, received, mine, *away):
    for bits in range(4):
        for half in range(2):
            slab = (place[0] ^ bits) * 2 + half
            total = keep[slab] + received[slab]
            if bits:
                away[bits - 1][half] = total.astype(BF16)
            else:
                mine[half] = total


def order_pairs(place, own, other, both):
    for k, bits in enumerate(ORDER):
        for j in range(4):
            y, z_lo = place[1] ^ bits, place[3] ^ j
            rows = pl.ds(pl.multiple_of((z_lo * 4 + y) * 112, 16), 112)
            both[k, pl.ds(j * 112, 112), :384] = own[rows]
            both[k, pl.ds(j * 112, 112), 384:] = other[rows]


def on_core(place, core):
    return pl.when(place[2] == core)


def by_x(*slabs):
    return jnp.concatenate([slab[j].reshape(448, 128) for slab in slabs for j in range(2)], 1)


def by_y(*slabs):
    halves = [jnp.concatenate([slab[j].reshape(448, 128) for slab in slabs]) for j in range(2)]
    return jnp.concatenate(halves, 1)


def rows(first, count=1):
    return pl.ds(first * 256, count * 256)


def deep(both, first, count):
    return both[pl.ds(first, count)].reshape(count * 448, 768)


def product_one(place, own, both, out):
    @on_core(place, 0)
    def _():
        out[...] = dot_t(by_x(own), both[0])

    @on_core(place, 1)
    def _():
        out[...] = dot_t(by_y(own), both[0])


def product_two(place, near1, near3, far, own1, near11, own3, near31, both, start, low, high):
    @on_core(place, 0)
    def _():
        total = dot_t(by_x(own1, near11), both[1]) + dot_t(by_x(own3, near31), both[2])
        low[rows(0)] = start[...] + total[:256]
        low[rows(1)] = dot_t(by_x(near1), both[0]) + total[256:]
        high[...] = dot_t(by_x(near3, far), both[0])

    @on_core(place, 1)
    def _():
        low[rows(0)] = start[...] + dot_t(by_y(near1, near3, far), deep(both, 1, 3))
        low[rows(1)] = dot_t(by_y(own1, near11), deep(both, 0, 2))
        high[rows(0)] = dot_t(by_y(own3, near31), deep(both, 0, 2))


def product_three(place, near31, far1, own, near1, both, low, mine, theirs):
    def keep(at, total):
        mine[at] = total[:, :384].astype(BF16)
        theirs[at] = total[:, 384:].astype(BF16)

    @on_core(place, 0)
    def _():
        keep(rows(0, 2), low[...] + dot_t(by_x(own, near1), both[3]))

    @on_core(place, 1)
    def _():
        keep(rows(0), low[rows(0)])
        keep(rows(1), low[rows(1)] + dot_t(by_y(near31, far1), deep(both, 2, 2)))


def product_four(place, near31, far1, near33, far3, both, start, high):
    @on_core(place, 0)
    def _():
        high[...] = (
            start[...] + dot_t(by_x(near31, far1), both[1]) + dot_t(by_x(near33, far3), both[2])
        )

    @on_core(place, 1)
    def _():
        high[rows(0)] = start[rows(0)] + dot_t(by_y(near33, far3), deep(both, 2, 2))


def product_five(side, place, own, near1, near3, far, both, high, out):
    columns = pl.ds(side * 384, 384)

    @on_core(place, 0)
    def _():
        total = high[:, columns] + dot_t(by_x(near3, far), both[3, :, columns])
        out[...] = total.astype(BF16)

    @on_core(place, 1)
    def _():
        out[rows(0)] = high[rows(0), columns].astype(BF16)
        left = by_y(own, near1, near3, far)
        out[rows(1)] = dot_t(left, both[:, :, columns].reshape(1792, 384)).astype(BF16)


def place_rows(place, mine1, mine2, theirs1, theirs2, out, sems):
    copies = []
    for block, core, which in (
        (mine1, place[2], 0),
        (mine2, place[2], 1),
        (theirs1, 1 - place[2], 0),
        (theirs2, 1 - place[2], 1),
    ):
        for i in range(2):
            row = core * 1024 + (place[0] ^ ORDER[which * 2 + i]) * 256
            at = pl.ds(pl.multiple_of(row, 256), 256)
            sem = sems.at[len(copies)]
            copies.append(pltpu.make_async_copy(block.at[rows(i)], out.at[at], sem))
    for copy in copies:
        copy.start()
    for copy in copies:
        copy.wait()


def call(kernel, out_shape, operands, out_specs=VMEM, specs=None, **more):
    return pl.pallas_call(
        kernel,
        out_shape=out_shape,
        in_specs=specs or [SMEM] + [VMEM] * (len(operands) - 1),
        out_specs=out_specs,
        compiler_params=PARAMS,
        cost_estimate=pl.CostEstimate(flops=0, bytes_accessed=0, transcendentals=0),
        **more,
    )(*operands)


def per_device(pair_valence, screening, pair_conduction):
    x, y, core, z_lo = (lax.axis_index(axis) for axis in ("x", "y", "core", "z_lo"))
    place = jnp.stack([x, y, core, z_lo]).astype(jnp.int32)

    slabs = jax.ShapeDtypeStruct((8, 112, 128), F32)
    keep, send = call(partial_sums, (slabs, slabs), (place, screening.astype(F32), pair_valence), (VMEM, VMEM))
    two = jax.ShapeDtypeStruct((2, 112, 128), F32)
    sent = jax.ShapeDtypeStruct((2, 112, 128), BF16)
    part, *away = call(
        add_cores,
        (two, sent, sent, sent),
        (place, keep, fetch(send, "core", 2, 1)),
        (VMEM,) * 4,
    )
    for bits in (3, 2, 1):
        part = part + swap(away[bits - 1], "x", 4, bits).astype(F32)

    other = fetch(pair_conduction, "core", 2, 1)
    both = call(
        order_pairs, jax.ShapeDtypeStruct((4, 448, 768), BF16), (place, pair_conduction, other)
    )

    share, both = lax.optimization_barrier((swap(part.astype(BF16), "z_hi", 2, 1), both))
    part = (part + share.astype(F32)).astype(BF16)
    own = jnp.stack([part] + [swap(part, "z_lo", 4, bits) for bits in (1, 2, 3)], 1)

    near1, near3 = turn(own, 0, 1), turn(own, 0, 3)
    total = jax.ShapeDtypeStruct((512, 768), F32)
    start = call(product_one, jax.ShapeDtypeStruct((256, 768), F32), (place, own, both))
    near1, start = lax.optimization_barrier((near1, start))
    far = turn(near1, 0, 3)
    one_own, three_own = turn(own, 1, 1), turn(own, 1, 3)
    one_near1, three_near1 = turn(near1, 1, 1), turn(near1, 1, 3)
    near3, one_own = lax.optimization_barrier((near3, one_own))
    one_near3, three_near3 = turn(near3, 1, 1), turn(near3, 1, 3)
    one_far, three_far = turn(far, 1, 1), turn(far, 1, 3)
    far_own, far_near1 = turn(three_own, 1, 1), turn(three_near1, 1, 1)
    far_near3, far_far = turn(one_near3, 1, 3), turn(one_far, 1, 3)
    low, high = call(
        product_two,
        (total, total),
        (place, near1, near3, far, one_own, one_near1, three_own, three_near1, both, start),
        (VMEM, VMEM),
    )
    high = call(
        product_four,
        total,
        (place, one_near3, one_far, three_near3, three_far, both, high),
    )
    far_near1, high = lax.optimization_barrier((far_near1, high))
    half = jax.ShapeDtypeStruct((512, 384), BF16)
    mine1, theirs1 = call(
        product_three,
        (half, half),
        (place, one_near3, one_far, far_own, far_near1, both, low),
        (VMEM, VMEM),
    )
    theirs1 = fetch(theirs1, "core", 2, 1)
    mine2, theirs2 = (
        call(
            functools.partial(product_five, side),
            half,
            (place, far_own, far_near1, far_near3, far_far, both, high),
        )
        for side in (0, 1)
    )
    theirs2 = fetch(theirs2, "core", 2, 1)
    return call(
        place_rows,
        jax.ShapeDtypeStruct((2048, 384), BF16),
        (place, mine1, mine2, theirs1, theirs2),
        ANY,
        scratch_shapes=[pltpu.SemaphoreType.DMA((8,))],
    )


def solution(mesh):
    fine = Mesh(mesh.devices.reshape(4, 2, 2, 4, 4), ROW + COL)
    placed = (P(ROW, None), P(ROW, COL), P(None, ROW + COL))
    return jax.shard_map(
        per_device, mesh=fine, in_specs=placed, out_specs=P(None, ROW + COL), check_vma=False
    )
```

```python
import functools
import itertools

import jax
import jax.numpy as jnp
from jax import lax
from jax.experimental import pallas as pl
from jax.experimental.pallas import tpu as pltpu
from jax.sharding import Mesh, PartitionSpec as P

ROW = ("x", "z_hi", "core")
COL = ("z_lo", "y")
Z = ("z_hi", "z_lo")
ORDER = (0, 1, 3, 2)
BF16 = jnp.bfloat16
F32 = jnp.float32
VMEM = pl.BlockSpec(memory_space=pltpu.VMEM)
SMEM = pl.BlockSpec(memory_space=pltpu.SMEM)
ANY = pl.BlockSpec(memory_space=pl.ANY)
PARAMS = pltpu.CompilerParams(vmem_limit_bytes=24 * 2**20)


def fetch(block, axis, size, ahead):
    return lax.ppermute(block, axis, [((i + ahead) % size, i) for i in range(size)])


def swap(block, axis, size, bits):
    return lax.ppermute(block, axis, [(i ^ bits, i) for i in range(size)])


def turn(block, order, bits):
    pairs = []
    for x, z_hi, core, z_lo, y in itertools.product(*map(range, (4, 2, 2, 4, 4))):
        source = (x ^ bits, y) if core == order else (x, y ^ bits)
        place = [((p * 2 + z_hi) * 2 + core) * 16 + z_lo * 4 + q for p, q in (source, (x, y))]
        pairs.append(tuple(place))
    return lax.ppermute(block, ROW + COL, pairs)


def dot_t(left, right):
    return lax.dot_general(left, right, (((0,), (0,)), ((), ())), preferred_element_type=F32)


def partial_sums(place, screening, panel, keep, send):
    core = place[2]
    for out, base in ((send, 1 - core), (keep, core)):
        for slab in range(8):
            columns = pl.ds(pl.multiple_of(base * 1024 + slab * 128, 128), 128)
            out[slab] = dot_t(screening[...], panel[:, columns])


def add_cores(place, keep, received, mine, *away):
    for bits in range(4):
        for half in range(2):
            slab = (place[0] ^ bits) * 2 + half
            total = keep[slab] + received[slab]
            if bits:
                away[bits - 1][half] = total.astype(BF16)
            else:
                mine[half] = total


def order_pairs(place, own, other, both):
    for k, bits in enumerate(ORDER):
        for j in range(4):
            y, z_lo = place[1] ^ bits, place[3] ^ j
            rows = pl.ds(pl.multiple_of((z_lo * 4 + y) * 112, 16), 112)
            both[k, pl.ds(j * 112, 112), :384] = own[rows]
            both[k, pl.ds(j * 112, 112), 384:] = other[rows]


def on_core(place, core):
    return pl.when(place[2] == core)


def by_x(*slabs):
    return jnp.concatenate([slab[j].reshape(448, 128) for slab in slabs for j in range(2)], 1)


def by_y(*slabs):
    halves = [jnp.concatenate([slab[j].reshape(448, 128) for slab in slabs]) for j in range(2)]
    return jnp.concatenate(halves, 1)


def rows(first, count=1):
    return pl.ds(first * 256, count * 256)


def deep(both, first, count):
    return both[pl.ds(first, count)].reshape(count * 448, 768)


def product_one(place, own, both, out):
    @on_core(place, 0)
    def _():
        out[...] = dot_t(by_x(own), both[0])

    @on_core(place, 1)
    def _():
        out[...] = dot_t(by_y(own), both[0])


def product_two(place, near1, near3, far, own1, near11, own3, near31, both, start, low, high):
    @on_core(place, 0)
    def _():
        total = dot_t(by_x(own1, near11), both[1]) + dot_t(by_x(own3, near31), both[2])
        low[rows(0)] = start[...] + total[:256]
        low[rows(1)] = dot_t(by_x(near1), both[0]) + total[256:]
        high[...] = dot_t(by_x(near3, far), both[0])

    @on_core(place, 1)
    def _():
        low[rows(0)] = start[...] + dot_t(by_y(near1, near3, far), deep(both, 1, 3))
        low[rows(1)] = dot_t(by_y(own1, near11), deep(both, 0, 2))
        high[rows(0)] = dot_t(by_y(own3, near31), deep(both, 0, 2))


def product_three(place, near31, far1, own, near1, both, low, mine, theirs):
    def keep(at, total):
        mine[at] = total[:, :384].astype(BF16)
        theirs[at] = total[:, 384:].astype(BF16)

    @on_core(place, 0)
    def _():
        keep(rows(0, 2), low[...] + dot_t(by_x(own, near1), both[3]))

    @on_core(place, 1)
    def _():
        keep(rows(0), low[rows(0)])
        keep(rows(1), low[rows(1)] + dot_t(by_y(near31, far1), deep(both, 2, 2)))


def product_four(place, near31, far1, near33, far3, both, start, high):
    @on_core(place, 0)
    def _():
        high[...] = (
            start[...] + dot_t(by_x(near31, far1), both[1]) + dot_t(by_x(near33, far3), both[2])
        )

    @on_core(place, 1)
    def _():
        high[rows(0)] = start[rows(0)] + dot_t(by_y(near33, far3), deep(both, 2, 2))


def product_five(side, place, own, near1, near3, far, both, high, out):
    columns = pl.ds(side * 384, 384)

    @on_core(place, 0)
    def _():
        total = high[:, columns] + dot_t(by_x(near3, far), both[3, :, columns])
        out[...] = total.astype(BF16)

    @on_core(place, 1)
    def _():
        out[rows(0)] = high[rows(0), columns].astype(BF16)
        left = by_y(own, near1, near3, far)
        out[rows(1)] = dot_t(left, both[:, :, columns].reshape(1792, 384)).astype(BF16)


def place_rows(place, mine1, mine2, theirs1, theirs2, out, sems):
    copies = []
    for block, core, which in (
        (mine1, place[2], 0),
        (mine2, place[2], 1),
        (theirs1, 1 - place[2], 0),
        (theirs2, 1 - place[2], 1),
    ):
        for i in range(2):
            row = core * 1024 + (place[0] ^ ORDER[which * 2 + i]) * 256
            at = pl.ds(pl.multiple_of(row, 256), 256)
            sem = sems.at[len(copies)]
            copies.append(pltpu.make_async_copy(block.at[rows(i)], out.at[at], sem))
    for copy in copies:
        copy.start()
    for copy in copies:
        copy.wait()


def call(kernel, out_shape, operands, out_specs=VMEM, specs=None, **more):
    return pl.pallas_call(
        kernel,
        out_shape=out_shape,
        in_specs=specs or [SMEM] + [VMEM] * (len(operands) - 1),
        out_specs=out_specs,
        compiler_params=PARAMS,
        cost_estimate=pl.CostEstimate(flops=0, bytes_accessed=0, transcendentals=0),
        **more,
    )(*operands)


def per_device(pair_valence, screening, pair_conduction):
    x, y, core, z_lo = (lax.axis_index(axis) for axis in ("x", "y", "core", "z_lo"))
    place = jnp.stack([x, y, core, z_lo]).astype(jnp.int32)

    slabs = jax.ShapeDtypeStruct((8, 112, 128), F32)
    keep, send = call(partial_sums, (slabs, slabs), (place, screening, pair_valence), (VMEM, VMEM))
    two = jax.ShapeDtypeStruct((2, 112, 128), F32)
    sent = jax.ShapeDtypeStruct((2, 112, 128), BF16)
    part, *away = call(
        add_cores,
        (two, sent, sent, sent),
        (place, keep, fetch(send, "core", 2, 1)),
        (VMEM,) * 4,
    )
    for bits in (3, 2, 1):
        part = part + swap(away[bits - 1], "x", 4, bits).astype(F32)

    other = fetch(pair_conduction, "core", 2, 1)
    both = call(
        order_pairs, jax.ShapeDtypeStruct((4, 448, 768), BF16), (place, pair_conduction, other)
    )

    share, both = lax.optimization_barrier((swap(part.astype(BF16), "z_hi", 2, 1), both))
    part = (part + share.astype(F32)).astype(BF16)
    own = jnp.stack([part] + [swap(part, "z_lo", 4, bits) for bits in (1, 2, 3)], 1)

    near1, near3 = turn(own, 0, 1), turn(own, 0, 3)
    total = jax.ShapeDtypeStruct((512, 768), F32)
    start = call(product_one, jax.ShapeDtypeStruct((256, 768), F32), (place, own, both))
    near1, start = lax.optimization_barrier((near1, start))
    far = turn(near1, 0, 3)
    one_own, three_own = turn(own, 1, 1), turn(own, 1, 3)
    near1, near3 = lax.optimization_barrier((near1, near3))
    one_near1, three_near1 = turn(near1, 1, 1), turn(near1, 1, 3)
    near3, one_own = lax.optimization_barrier((near3, one_own))
    one_near3, three_near3 = turn(near3, 1, 1), turn(near3, 1, 3)
    one_far, three_far = turn(far, 1, 1), turn(far, 1, 3)
    far_own, far_near1 = turn(three_own, 1, 1), turn(three_near1, 1, 1)
    far_near3, far_far = turn(one_near3, 1, 3), turn(one_far, 1, 3)
    low, high = call(
        product_two,
        (total, total),
        (place, near1, near3, far, one_own, one_near1, three_own, three_near1, both, start),
        (VMEM, VMEM),
    )
    high = call(
        product_four,
        total,
        (place, one_near3, one_far, three_near3, three_far, both, high),
    )
    far_near1, high = lax.optimization_barrier((far_near1, high))
    half = jax.ShapeDtypeStruct((512, 384), BF16)
    mine1, theirs1 = call(
        product_three,
        (half, half),
        (place, one_near3, one_far, far_own, far_near1, both, low),
        (VMEM, VMEM),
    )
    theirs1 = fetch(theirs1, "core", 2, 1)
    mine2, theirs2 = (
        call(
            functools.partial(product_five, side),
            half,
            (place, far_own, far_near1, far_near3, far_far, both, high),
        )
        for side in (0, 1)
    )
    theirs2 = fetch(theirs2, "core", 2, 1)
    return call(
        place_rows,
        jax.ShapeDtypeStruct((2048, 384), BF16),
        (place, mine1, mine2, theirs1, theirs2),
        ANY,
        scratch_shapes=[pltpu.SemaphoreType.DMA((8,))],
    )


def solution(mesh):
    fine = Mesh(mesh.devices.reshape(4, 2, 2, 4, 4), ROW + COL)
    placed = (P(ROW, None), P(ROW, COL), P(None, ROW + COL))
    return jax.shard_map(
        per_device, mesh=fine, in_specs=placed, out_specs=P(None, ROW + COL), check_vma=False
    )
```

```python
import functools
import itertools

import jax
import jax.numpy as jnp
from jax import lax
from jax.experimental import pallas as pl
from jax.experimental.pallas import tpu as pltpu
from jax.sharding import Mesh, PartitionSpec as P

ROW = ("x", "z_hi", "core")
COL = ("z_lo", "y")
Z = ("z_hi", "z_lo")
ORDER = (0, 1, 3, 2)
BF16 = jnp.bfloat16
F32 = jnp.float32
VMEM = pl.BlockSpec(memory_space=pltpu.VMEM)
SMEM = pl.BlockSpec(memory_space=pltpu.SMEM)
ANY = pl.BlockSpec(memory_space=pl.ANY)
PARAMS = pltpu.CompilerParams(vmem_limit_bytes=24 * 2**20)


def fetch(block, axis, size, ahead):
    return lax.ppermute(block, axis, [((i + ahead) % size, i) for i in range(size)])


def swap(block, axis, size, bits):
    return lax.ppermute(block, axis, [(i ^ bits, i) for i in range(size)])


def turn(block, order, bits):
    pairs = []
    for x, z_hi, core, z_lo, y in itertools.product(*map(range, (4, 2, 2, 4, 4))):
        source = (x ^ bits, y) if core == order else (x, y ^ bits)
        place = [((p * 2 + z_hi) * 2 + core) * 16 + z_lo * 4 + q for p, q in (source, (x, y))]
        pairs.append(tuple(place))
    return lax.ppermute(block, ROW + COL, pairs)


def dot_t(left, right):
    return lax.dot_general(left, right, (((0,), (0,)), ((), ())), preferred_element_type=F32)


def partial_sums(place, screening, panel, keep, send):
    core = place[2]
    for out, base in ((send, 1 - core), (keep, core)):
        for slab in range(8):
            columns = pl.ds(pl.multiple_of(base * 1024 + slab * 128, 128), 128)
            out[slab] = dot_t(screening[...], panel[:, columns])


def add_cores(place, keep, received, mine, *away):
    for bits in range(4):
        for half in range(2):
            slab = (place[0] ^ bits) * 2 + half
            total = keep[slab] + received[slab]
            if bits:
                away[bits - 1][half] = total.astype(BF16)
            else:
                mine[half] = total


def order_pairs(place, own, other, both):
    for k, bits in enumerate(ORDER):
        for j in range(4):
            y, z_lo = place[1] ^ bits, place[3] ^ j
            rows = pl.ds(pl.multiple_of((z_lo * 4 + y) * 112, 16), 112)
            both[k, pl.ds(j * 112, 112), :384] = own[rows]
            both[k, pl.ds(j * 112, 112), 384:] = other[rows]


def on_core(place, core):
    return pl.when(place[2] == core)


def by_x(*slabs):
    return jnp.concatenate([slab[j].reshape(448, 128) for slab in slabs for j in range(2)], 1)


def by_y(*slabs):
    halves = [jnp.concatenate([slab[j].reshape(448, 128) for slab in slabs]) for j in range(2)]
    return jnp.concatenate(halves, 1)


def rows(first, count=1):
    return pl.ds(first * 256, count * 256)


def deep(both, first, count):
    return both[pl.ds(first, count)].reshape(count * 448, 768)


def product_one(place, own, both, out):
    @on_core(place, 0)
    def _():
        out[...] = dot_t(by_x(own), both[0])

    @on_core(place, 1)
    def _():
        out[...] = dot_t(by_y(own), both[0])


def product_two(place, near1, near3, far, own1, near11, own3, near31, both, start, low, high):
    @on_core(place, 0)
    def _():
        total = dot_t(by_x(own1, near11), both[1]) + dot_t(by_x(own3, near31), both[2])
        low[rows(0)] = start[...] + total[:256]
        low[rows(1)] = dot_t(by_x(near1), both[0]) + total[256:]
        high[...] = dot_t(by_x(near3, far), both[0])

    @on_core(place, 1)
    def _():
        low[rows(0)] = start[...] + dot_t(by_y(near1, near3, far), deep(both, 1, 3))
        low[rows(1)] = dot_t(by_y(own1, near11), deep(both, 0, 2))
        high[rows(0)] = dot_t(by_y(own3, near31), deep(both, 0, 2))


def product_three(place, near31, far1, own, near1, both, low, mine, theirs):
    def keep(at, total):
        mine[at] = total[:, :384].astype(BF16)
        theirs[at] = total[:, 384:].astype(BF16)

    @on_core(place, 0)
    def _():
        keep(rows(0, 2), low[...] + dot_t(by_x(own, near1), both[3]))

    @on_core(place, 1)
    def _():
        keep(rows(0), low[rows(0)])
        keep(rows(1), low[rows(1)] + dot_t(by_y(near31, far1), deep(both, 2, 2)))


def product_four(place, near31, far1, near33, far3, both, start, high):
    @on_core(place, 0)
    def _():
        high[...] = (
            start[...] + dot_t(by_x(near31, far1), both[1]) + dot_t(by_x(near33, far3), both[2])
        )

    @on_core(place, 1)
    def _():
        high[rows(0)] = start[rows(0)] + dot_t(by_y(near33, far3), deep(both, 2, 2))


def product_five(side, place, own, near1, near3, far, both, high, out):
    columns = pl.ds(side * 384, 384)

    @on_core(place, 0)
    def _():
        total = high[:, columns] + dot_t(by_x(near3, far), both[3, :, columns])
        out[...] = total.astype(BF16)

    @on_core(place, 1)
    def _():
        out[rows(0)] = high[rows(0), columns].astype(BF16)
        left = by_y(own, near1, near3, far)
        out[rows(1)] = dot_t(left, both[:, :, columns].reshape(1792, 384)).astype(BF16)


def place_rows(place, mine1, mine2, theirs1, theirs2, out, sems):
    copies = []
    for block, core, which in (
        (mine1, place[2], 0),
        (mine2, place[2], 1),
        (theirs1, 1 - place[2], 0),
        (theirs2, 1 - place[2], 1),
    ):
        for i in range(2):
            row = core * 1024 + (place[0] ^ ORDER[which * 2 + i]) * 256
            at = pl.ds(pl.multiple_of(row, 256), 256)
            sem = sems.at[len(copies)]
            copies.append(pltpu.make_async_copy(block.at[rows(i)], out.at[at], sem))
    for copy in copies:
        copy.start()
    for copy in copies:
        copy.wait()


def call(kernel, out_shape, operands, out_specs=VMEM, specs=None, **more):
    return pl.pallas_call(
        kernel,
        out_shape=out_shape,
        in_specs=specs or [SMEM] + [VMEM] * (len(operands) - 1),
        out_specs=out_specs,
        compiler_params=PARAMS,
        cost_estimate=pl.CostEstimate(flops=0, bytes_accessed=0, transcendentals=0),
        **more,
    )(*operands)


def per_device(pair_valence, screening, pair_conduction):
    x, y, core, z_lo = (lax.axis_index(axis) for axis in ("x", "y", "core", "z_lo"))
    place = jnp.stack([x, y, core, z_lo]).astype(jnp.int32)

    slabs = jax.ShapeDtypeStruct((8, 112, 128), F32)
    keep, send = call(partial_sums, (slabs, slabs), (place, screening, pair_valence), (VMEM, VMEM))
    two = jax.ShapeDtypeStruct((2, 112, 128), F32)
    sent = jax.ShapeDtypeStruct((2, 112, 128), BF16)
    part, *away = call(
        add_cores,
        (two, sent, sent, sent),
        (place, keep, fetch(send, "core", 2, 1)),
        (VMEM,) * 4,
    )
    for bits in (3, 2, 1):
        part = part + swap(away[bits - 1], "x", 4, bits).astype(F32)

    other = fetch(pair_conduction, "core", 2, 1)
    both = call(
        order_pairs, jax.ShapeDtypeStruct((4, 448, 768), BF16), (place, pair_conduction, other)
    )

    share, both = lax.optimization_barrier((swap(part.astype(BF16), "z_hi", 2, 1), both))
    part = (part + share.astype(F32)).astype(BF16)
    own = jnp.stack([part] + [swap(part, "z_lo", 4, bits) for bits in (1, 2, 3)], 1)

    near1, near3 = turn(own, 0, 1), turn(own, 0, 3)
    total = jax.ShapeDtypeStruct((512, 768), F32)
    start = call(product_one, jax.ShapeDtypeStruct((256, 768), F32), (place, own, both))
    far = turn(near1, 0, 3)
    one_own, three_own = turn(own, 1, 1), turn(own, 1, 3)
    near1, near3, start = lax.optimization_barrier((near1, near3, start))
    one_near1, three_near1 = turn(near1, 1, 1), turn(near1, 1, 3)
    one_near3, three_near3 = turn(near3, 1, 1), turn(near3, 1, 3)
    one_far, three_far = turn(far, 1, 1), turn(far, 1, 3)
    far_own, far_near1 = turn(three_own, 1, 1), turn(three_near1, 1, 1)
    far_near3, far_far = turn(one_near3, 1, 3), turn(one_far, 1, 3)
    low, high = call(
        product_two,
        (total, total),
        (place, near1, near3, far, one_own, one_near1, three_own, three_near1, both, start),
        (VMEM, VMEM),
    )
    high = call(
        product_four,
        total,
        (place, one_near3, one_far, three_near3, three_far, both, high),
    )
    far_near1, high = lax.optimization_barrier((far_near1, high))
    half = jax.ShapeDtypeStruct((512, 384), BF16)
    mine1, theirs1 = call(
        product_three,
        (half, half),
        (place, one_near3, one_far, far_own, far_near1, both, low),
        (VMEM, VMEM),
    )
    theirs1 = fetch(theirs1, "core", 2, 1)
    mine2, theirs2 = (
        call(
            functools.partial(product_five, side),
            half,
            (place, far_own, far_near1, far_near3, far_far, both, high),
        )
        for side in (0, 1)
    )
    theirs2 = fetch(theirs2, "core", 2, 1)
    return call(
        place_rows,
        jax.ShapeDtypeStruct((2048, 384), BF16),
        (place, mine1, mine2, theirs1, theirs2),
        ANY,
        scratch_shapes=[pltpu.SemaphoreType.DMA((8,))],
    )


def solution(mesh):
    fine = Mesh(mesh.devices.reshape(4, 2, 2, 4, 4), ROW + COL)
    placed = (P(ROW, None), P(ROW, COL), P(None, ROW + COL))
    return jax.shard_map(
        per_device, mesh=fine, in_specs=placed, out_specs=P(None, ROW + COL), check_vma=False
    )
```
